256 devices in a mesh: space: 64 (over y_lo, z, x), snap: 4 (over y_hi, core).
Axes of the slice: x: 4, y: 4 (y_hi: 2, y_lo: 2; y = y_hi * 2 + y_lo), z: 8, core: 2. Of those that a mesh axis runs over, the one named last changes fastest.
Arguments:
- snapshots: bfloat16 [64, 3, 128, 64, 128], P('snap', None, 'space'), may hold values from -8 to 8
- labels: int32 [128, 64, 128], P('space'), may hold values from 0 to 2
- free_mask: int32 [128, 64, 128], P('space'), may hold values 0 or 1
- density: float32 [3], replicated, may hold values from 0.5 to 2
Outputs:
- grams: float32 [4, 64, 64], P(None, 'space')
- slab_grams: float32 [64, 4, 64, 64], P('space')
The draws below stay inside these ranges and needn't reach their ends.
All inputs are finite; a program needn't handle non-finite values. No bound on the sum of `free_mask` on one device may be relied on, other than what follows from the above.
Results may differ from the reference program's by a relative error of at most 0.0003.
Values may be sent and summed in bfloat16 or wider, within the bound.
No kernel may reach another device: no remote copies, remote signals or barrier semaphores. Data moves between devices by JAX's collectives and lax.ppermute only.
A program may use at most 128 MiB of HBM per device.

```python
import math
import jax
import jax.numpy as jnp
from jax import lax

S = 64
NMAT = 3
CX = 2
NY = 64
NZ = 128
NX = 128


def draw_snapshots(key, part):
    key_mix = jax.random.fold_in(key, 0)
    key_field = jax.random.fold_in(key, 1)
    key_noise = jax.random.fold_in(key, 2)
    key_gain = jax.random.fold_in(key, 4)
    key_box = jax.random.fold_in(key, 5)
    mixing = jax.random.normal(key_mix, (S, 8), jnp.float32) * 0.6
    fields = jax.random.normal(key_field, (8, 3, NX, NY, NZ), jnp.float32)
    ramp = 0.5 + 1.5 * (jnp.arange(NX, dtype=jnp.float32) + 0.5) / NX
    gain_x = jnp.exp(jax.random.uniform(jax.random.fold_in(key_gain, 0), (NX,), jnp.float32, -0.5, 0.5))
    gain_y = jnp.exp(jax.random.uniform(jax.random.fold_in(key_gain, 1), (NY,), jnp.float32, -0.5, 0.5))
    gain_z = jnp.exp(jax.random.uniform(jax.random.fold_in(key_gain, 2), (NZ,), jnp.float32, -0.5, 0.5))
    rough = 0.45 * (ramp * gain_x)[:, None, None] * gain_y[None, :, None] * gain_z[None, None, :]
    pos_x = jnp.arange(NX, dtype=jnp.int32)[:, None, None]
    pos_y = jnp.arange(NY, dtype=jnp.int32)[None, :, None]
    pos_z = jnp.arange(NZ, dtype=jnp.int32)[None, None, :]

    def one_snapshot(member):
        noise = jax.random.normal(jax.random.fold_in(key_noise, member), (3, NX, NY, NZ), jnp.float32)
        mixed = noise
        for source in range(8):
            mixed = mixed + mixing[member, source] * fields[source]
        key_bx, key_by, key_bz = jax.random.split(jax.random.fold_in(key_box, member), 3)
        start_x = jax.random.randint(key_bx, (), 0, NX - NX // 2 + 1)
        start_y = jax.random.randint(key_by, (), 0, NY - NY // 2 + 1)
        start_z = jax.random.randint(key_bz, (), 0, NZ - NZ // 2 + 1)
        inside = (pos_x >= start_x) & (pos_x < start_x + NX // 2)
        inside = inside & (pos_y >= start_y) & (pos_y < start_y + NY // 2)
        inside = inside & (pos_z >= start_z) & (pos_z < start_z + NZ // 2)
        envelope = 0.5 + inside.astype(jnp.float32)
        values = mixed * (rough * envelope)[None]
        return jnp.clip(values, -8.0, 8.0).astype(jnp.bfloat16)
    return lax.map(one_snapshot, jnp.arange(S, dtype=jnp.int32))


def set_ends(entries, key, low, top_value):
    longest = entries.shape.index(max(entries.shape))
    spots = []
    for shift in (0, 1):
        where = [jax.random.randint(jax.random.fold_in(key, axis), (), 0, length) for axis, length in enumerate(entries.shape)]
        where[longest] = (where[longest] + shift) % entries.shape[longest]
        spots.append(tuple(where))
    return entries.at[spots[0]].set(low).at[spots[1]].set(top_value)


def setup_inputs(seed: int = 0) -> dict:
    seeds = jax.random.split(jax.random.key(seed), 5)
    snapshots = draw_snapshots(jax.random.fold_in(seeds[4], 71), 0)
    labels = set_ends(jax.random.randint(seeds[1], (NX, NY, NZ), 0, NMAT), jax.random.fold_in(seeds[1], 1), 0, NMAT - 1).astype(jnp.int32)
    free_mask = set_ends((jax.random.randint(seeds[2], (NX, NY, NZ), 0, 16) < 15).astype(jnp.int32), jax.random.fold_in(seeds[2], 1), 0, 1)
    density = jnp.clip(jnp.exp(jax.random.uniform(seeds[3], (NMAT,), jnp.float32, math.log(0.5), math.log(2.0))), 0.5, 2.0)
    return {"snapshots": snapshots, "labels": labels, "free_mask": free_mask, "density": density}


def mass_line(values, axis_dim):
    length = values.shape[axis_dim]
    before = lax.slice_in_dim(values, 0, length - 2, axis=axis_dim)
    centre = lax.slice_in_dim(values, 1, length - 1, axis=axis_dim)
    behind = lax.slice_in_dim(values, 2, length, axis=axis_dim)
    return (before + 4.0 * centre + behind) * (1.0 / 6.0)


def stiff_line(values, axis_dim):
    length = values.shape[axis_dim]
    before = lax.slice_in_dim(values, 0, length - 2, axis=axis_dim)
    centre = lax.slice_in_dim(values, 1, length - 1, axis=axis_dim)
    behind = lax.slice_in_dim(values, 2, length, axis=axis_dim)
    return 2.0 * centre - before - behind


def images(padded, density_field):
    values = padded.astype(jnp.float32)
    mass_x = mass_line(values, 2)
    stiff_x = stiff_line(values, 2)
    mass_xy = mass_line(mass_x, 3)
    mixed_xy = stiff_line(mass_x, 3)
    stiff_xy = mass_line(stiff_x, 3)
    mass_full = mass_line(mass_xy, 4)
    stiff_full = stiff_line(mass_xy, 4) + mass_line(mixed_xy, 4) + mass_line(stiff_xy, 4)
    return (density_field * mass_full).astype(jnp.bfloat16), stiff_full.astype(jnp.bfloat16)


def density_of(cell_labels, density):
    density_field = jnp.zeros(cell_labels.shape, jnp.float32)
    for material in range(density.shape[0]):
        density_field = density_field + jnp.where(cell_labels == material, density[material], 0.0)
    return density_field


def stacked_images(mass_img, stiff_img, cell_labels, materials):
    zero_value = jnp.zeros((), stiff_img.dtype)
    blocks = [mass_img] + [jnp.where(cell_labels == material, stiff_img, zero_value) for material in range(materials)]
    stacked = jnp.stack(blocks)
    return stacked.reshape(stacked.shape[0] * stacked.shape[1], -1)


def reference(snapshots, labels, free_mask, density):
    masked = snapshots * free_mask.astype(jnp.bfloat16)[None, None]
    padded = jnp.pad(masked, ((0, 0), (0, 0), (1, 1), (1, 1), (1, 1)))

    def accumulate(summed, block_index):
        offset = block_index * CX
        block = lax.dynamic_slice_in_dim(padded, offset, CX + 2, 2)
        inner = lax.dynamic_slice_in_dim(masked, offset, CX, 2)
        cell_labels = lax.dynamic_slice_in_dim(labels, offset, CX, 0)
        mass_img, stiff_img = images(block, density_of(cell_labels, density))
        stacked = stacked_images(mass_img, stiff_img, cell_labels, NMAT)
        flat_snaps = inner.reshape(S, -1)
        product = jnp.dot(flat_snaps, stacked.T, preferred_element_type=jnp.float32)
        product = product.reshape(S, NMAT + 1, S).transpose(1, 0, 2)
        return summed + product, product

    start_value = jnp.zeros((NMAT + 1, S, S), jnp.float32)
    summed, tiles = lax.scan(accumulate, start_value, jnp.arange(NX // CX, dtype=jnp.int32))
    grams = summed * (1.0 / (3.0 * NX * NY * NZ))
    slab_grams = tiles * (1.0 / (3.0 * CX * NY * NZ))
    return grams, slab_grams
```

```python
import functools

import jax
import jax.numpy as jnp
import numpy as np
from jax import lax
from jax.experimental import pallas as pl
from jax.experimental.pallas import tpu as pltpu
from jax.sharding import PartitionSpec as P


def spread_kernel(groups, width, me_ref, snaps_ref, mask_ref, *refs):
    outs, turned = refs[:groups], refs[groups]
    rows = snaps_ref.shape[3]
    me = me_ref[0]
    mask = mask_ref[0].astype(jnp.float32)
    values = snaps_ref[:, 0, 0].astype(jnp.float32) * mask[None]
    edge = jnp.zeros(turned.shape[1:], turned.dtype)
    turned[0] = edge
    turned[rows + 1] = edge
    turned[1 : rows + 1] = jnp.swapaxes(values, 0, 1).astype(turned.dtype)
    for m in range(groups):
        outs[m][0, 0] = turned[pl.ds((me ^ m) * width, width + 2)]


def spread(snapshots, free_mask, me, groups):
    members, comps, planes, rows, depth = snapshots.shape
    width = rows // groups
    block = jax.ShapeDtypeStruct((comps, planes, width + 2, members, depth), snapshots.dtype)
    out_spec = pl.BlockSpec((1, 1, width + 2, members, depth), lambda c, p, me: (c, p, 0, 0, 0))
    return pl.pallas_call(
        functools.partial(spread_kernel, groups, width),
        out_shape=[block] * groups,
        grid_spec=pltpu.PrefetchScalarGridSpec(
            num_scalar_prefetch=1,
            grid=(comps, planes),
            in_specs=[
                pl.BlockSpec((members, 1, 1, rows, depth), lambda c, p, me: (0, c, p, 0, 0)),
                pl.BlockSpec((1, rows, depth), lambda c, p, me: (p, 0, 0)),
            ],
            out_specs=[out_spec] * groups,
            scratch_shapes=[pltpu.VMEM((rows + 2, members, depth), snapshots.dtype)],
        ),
        compiler_params=pltpu.CompilerParams(vmem_limit_bytes=32 * 2**20),
        cost_estimate=pl.CostEstimate(flops=0, bytes_accessed=5 * 2**20, transcendentals=0),
    )(me, snapshots, free_mask)


def stencil_weights(depth):
    mass = {-1: 1.0, 0: 4.0, 1: 1.0}
    stiff = {-1: -1.0, 0: 2.0, 1: -1.0}
    near = np.eye(depth, k=1) + np.eye(depth, k=-1)
    mass_z = 4.0 * np.eye(depth) + near
    stiff_z = 2.0 * np.eye(depth) - near
    blocks = []
    for dx in (-1, 0, 1):
        for dy in (-1, 0, 1):
            both = mass[dx] * mass[dy]
            mixed = stiff[dx] * mass[dy] + mass[dx] * stiff[dy]
            blocks.append(np.concatenate([both * mass_z, mixed * mass_z + both * stiff_z], axis=1))
    return np.concatenate(blocks, axis=0)


def tiles_kernel(groups, materials, me_ref, density_ref, *refs):
    sources = refs[:groups]
    low_ref, high_ref, labels_ref, weights_ref, part_ref, wide_ref, left, right = refs[groups:]
    comp = pl.program_id(0)
    me = me_ref[0]
    planes, reach, members, depth = sources[0].shape[1:]
    width = reach - 2
    count = groups * members

    @pl.when(comp == 0)
    def _():
        part_ref[...] = jnp.zeros_like(part_ref)

    for p in range(planes):
        shifted = []
        for m in range(groups):
            pieces = []
            for dx in (-1, 0, 1):
                at = p + dx
                plane = low_ref.at[0, m] if at < 0 else high_ref.at[0, m] if at >= planes else sources[m].at[0, at]
                for dy in range(3):
                    pieces.append(plane[dy : dy + width].reshape(width * members, depth))
            shifted.append(jnp.concatenate(pieces, axis=1))
        image = jnp.dot(
            jnp.concatenate(shifted, axis=0), weights_ref[...], preferred_element_type=jnp.float32
        )
        mass = image[:, :depth].reshape(groups, width, members, depth)
        stiff = image[:, depth:].reshape(groups, width, members, depth) * (1.0 / 36.0)
        for y in range(width):
            label = labels_ref[p, pl.ds(me * width + y, 1), :]
            density = jnp.zeros(label.shape, jnp.float32)
            for j in range(materials):
                density = density + jnp.where(label == j, density_ref[j] * (1.0 / 216.0), 0.0)
            lanes = slice((p * width + y) * depth, (p * width + y + 1) * depth)
            for m in range(groups):
                start = pl.multiple_of((me ^ m) * members, members)
                left[pl.ds(start, members), lanes] = sources[m][0, p, y + 1]
                right[pl.ds(start, members), lanes] = (mass[m, y] * density).astype(right.dtype)
                for j in range(materials):
                    at = pl.multiple_of((j + 1) * count + start, members)
                    right[pl.ds(at, members), lanes] = jnp.where(label == j, stiff[m, y], 0.0).astype(right.dtype)
    part_ref[...] += lax.dot_general(
        left[...], right[...], (((1,), (1,)), ((), ())), preferred_element_type=jnp.float32
    )

    @pl.when(comp == pl.num_programs(0) - 1)
    def _():
        for s in range(count):
            row = part_ref[pl.ds(s, 1), :]
            wide_ref[pl.ds(s * groups, groups), :] = jnp.broadcast_to(row, (groups, row.shape[1]))


def tiles(blocks, low, high, labels, density, me):
    groups = len(blocks)
    comps, planes, reach, members, depth = blocks[0].shape
    materials = density.shape[0]
    count = groups * members
    cells = planes * (reach - 2) * depth
    columns = (materials + 1) * count
    weights = jnp.asarray(stencil_weights(depth), jnp.bfloat16)
    block = pl.BlockSpec((1, planes, reach, members, depth), lambda c, *_: (c, 0, 0, 0, 0))
    halo = pl.BlockSpec((1, groups, reach, members, depth), lambda c, *_: (c, 0, 0, 0, 0))
    whole = lambda a: pl.BlockSpec(a.shape, lambda c, *_: (0,) * a.ndim)
    part = jax.ShapeDtypeStruct((count, columns), jnp.float32)
    wide = jax.ShapeDtypeStruct((count * groups, columns), jnp.float32)
    return pl.pallas_call(
        functools.partial(tiles_kernel, groups, materials),
        out_shape=[part, wide],
        grid_spec=pltpu.PrefetchScalarGridSpec(
            num_scalar_prefetch=2,
            grid=(comps,),
            in_specs=[block] * groups + [halo, halo, whole(labels), whole(weights)],
            out_specs=[whole(part), whole(wide)],
            scratch_shapes=[
                pltpu.VMEM((count, cells), jnp.bfloat16),
                pltpu.VMEM((columns, cells), jnp.bfloat16),
            ],
        ),
        compiler_params=pltpu.CompilerParams(vmem_limit_bytes=48 * 2**20),
        cost_estimate=pl.CostEstimate(flops=5 * 10**9, bytes_accessed=5 * 2**20, transcendentals=0),
    )(me, density, *blocks, low, high, labels, weights)


def finish_kernel(count, slab_scale, gram_scale, *refs):
    parts, rows_ref, slab_ref, gram_ref = refs[:-3], refs[-3], refs[-2], refs[-1]
    terms = [p[...] for p in parts]
    while len(terms) > 1:
        terms = [terms[i] + terms[i + 1] for i in range(0, len(terms), 2)]
    slab = terms[0] * slab_scale
    gram = jnp.sum(rows_ref[...], axis=0, keepdims=True) * gram_scale
    for j in range(slab.shape[1] // count):
        slab_ref[0, j] = slab[:, j * count : (j + 1) * count]
        gram_ref[j] = gram[:, j * count : (j + 1) * count]


def finish(parts, rows, slab_scale, gram_scale):
    count, columns = parts[0].shape
    blocks = columns // count
    return pl.pallas_call(
        functools.partial(finish_kernel, count, slab_scale, gram_scale),
        out_shape=[
            jax.ShapeDtypeStruct((1, blocks, count, count), jnp.float32),
            jax.ShapeDtypeStruct((blocks, 1, count), jnp.float32),
        ],
    )(*parts, rows)


def body(snapshots, labels, free_mask, density):
    groups, slabs = lax.axis_size("snap"), lax.axis_size("space")
    planes, rows, depth = labels.shape
    me = lax.axis_index("snap").astype(jnp.int32).reshape(1)
    with jax.named_scope("spread"):
        mine = spread(snapshots, free_mask, me, groups)
    with jax.named_scope("regroup"):
        blocks = [mine[0]] + [
            lax.ppermute(mine[m], "snap", [(i, i ^ m) for i in range(groups)]) for m in range(1, groups)
        ]
    with jax.named_scope("halo"):
        forward = [(i, i + 1) for i in range(slabs - 1)]
        backward = [(b, a) for a, b in forward]
        low = lax.ppermute(jnp.stack([b[:, planes - 1] for b in blocks], axis=1), "space", forward)
        high = lax.ppermute(jnp.stack([b[:, 0] for b in blocks], axis=1), "space", backward)
    with jax.named_scope("tiles"):
        part, wide = tiles(blocks, low, high, labels, density, me)
    with jax.named_scope("sums"):
        parts = [part] + [
            lax.ppermute(part, "snap", [(i, i ^ m) for i in range(groups)]) for m in range(1, groups)
        ]
        sent = lax.all_to_all(wide, ("space", "snap"), 0, 0, tiled=True)
        slab_scale = 1.0 / (3.0 * planes * rows * depth)
        slab, gram = finish(parts, sent, slab_scale, slab_scale / slabs)
    return gram, slab


def solution(mesh):
    in_specs = (
        P("snap", None, "space", None, None),
        P("space", None, None),
        P("space", None, None),
        P(),
    )
    out_specs = (P(None, "space", None), P("space", None, None, None))
    return jax.shard_map(body, mesh=mesh, in_specs=in_specs, out_specs=out_specs, check_vma=False)
```

```python
import functools

import jax
import jax.numpy as jnp
import numpy as np
from jax import lax
from jax.experimental import pallas as pl
from jax.experimental.pallas import tpu as pltpu
from jax.sharding import PartitionSpec as P


def spread_kernel(groups, me_ref, snaps_ref, mask_ref, *refs):
    outs, (held, mask, turned, sems) = refs[:groups], refs[groups:]
    comps, planes, reach = outs[0].shape[:3]
    width = reach - 2
    rows = groups * width
    me = me_ref[0]
    steps = [(c, p) for c in range(comps) for p in range(planes)]
    mask_copy = pltpu.make_async_copy(mask_ref, mask, sems.at[len(steps)])
    mask_copy.start()
    copies = [
        pltpu.make_async_copy(snaps_ref.at[:, c, p], held.at[i], sems.at[i]) for i, (c, p) in enumerate(steps)
    ]
    for copy in copies:
        copy.start()
    edge = jnp.zeros(turned.shape[1:], turned.dtype)
    turned[0] = edge
    turned[rows + 1] = edge
    mask_copy.wait()
    for i, (c, p) in enumerate(steps):
        copies[i].wait()
        values = held[i].astype(jnp.float32) * mask[p].astype(jnp.float32)[None]
        turned[1 : rows + 1] = jnp.swapaxes(values, 0, 1).astype(turned.dtype)
        for m in range(groups):
            outs[m][c, p] = turned[pl.ds((me ^ m) * width, reach)]


def spread(snapshots, free_mask, me, groups):
    members, comps, planes, rows, depth = snapshots.shape
    block = jax.ShapeDtypeStruct((comps, planes, rows // groups + 2, members, depth), snapshots.dtype)
    hbm = pl.BlockSpec(memory_space=pltpu.HBM)
    return pl.pallas_call(
        functools.partial(spread_kernel, groups),
        out_shape=[block] * groups,
        in_specs=[smem_spec(), hbm, hbm],
        out_specs=[vmem_spec()] * groups,
        scratch_shapes=[
            pltpu.VMEM((comps * planes, members, rows, depth), snapshots.dtype),
            pltpu.VMEM(free_mask.shape, free_mask.dtype),
            pltpu.VMEM((rows + 2, members, depth), snapshots.dtype),
            pltpu.SemaphoreType.DMA((comps * planes + 1,)),
        ],
        compiler_params=pltpu.CompilerParams(vmem_limit_bytes=16 * 2**20),
        cost_estimate=pl.CostEstimate(flops=0, bytes_accessed=5 * 2**20, transcendentals=0),
    )(me, snapshots, free_mask)


def stencil_weights(depth):
    mass = {-1: 1.0, 0: 4.0, 1: 1.0}
    stiff = {-1: -1.0, 0: 2.0, 1: -1.0}
    near = np.eye(depth, k=1) + np.eye(depth, k=-1)
    mass_z = 4.0 * np.eye(depth) + near
    stiff_z = 2.0 * np.eye(depth) - near

    def plane(dx):
        blocks = []
        for dy in (-1, 0, 1):
            both = mass[dx] * mass[dy]
            mixed = stiff[dx] * mass[dy] + mass[dx] * stiff[dy]
            blocks.append(np.concatenate([both * mass_z, mixed * mass_z + both * stiff_z], axis=1))
        return np.concatenate(blocks, axis=0)

    return plane(0), plane(1)


def three_rows(block, first, height):
    members, depth = block.shape[-2:]
    return [block[first + dy : first + dy + height].reshape(height * members, depth) for dy in range(3)]


def density_at(label, density_ref, materials):
    density = jnp.zeros(label.shape, jnp.float32)
    for j in range(materials):
        density = density + jnp.where(label == j, density_ref[j] * (1.0 / 216.0), 0.0)
    return density


def put_images(image, label, density, right, start, lanes, count, materials):
    members, depth = image.shape[0], image.shape[1] // 2
    right[pl.ds(start, members), lanes] = (image[:, :depth] * density).astype(right.dtype)
    stiff = image[:, depth:] * (1.0 / 36.0)
    for j in range(materials):
        at = pl.multiple_of((j + 1) * count + start, members)
        right[pl.ds(at, members), lanes] = jnp.where(label == j, stiff, 0.0).astype(right.dtype)


def correlate(left, right):
    return lax.dot_general(left, right, (((1,), (1,)), ((), ())), preferred_element_type=jnp.float32)


def local_kernel(groups, materials, me_ref, density_ref, *refs):
    sources = refs[:groups]
    labels_ref, weights_ref, part_ref, edge_ref, cross_ref, left_ref, near_left, near_right = refs[groups:]
    me = me_ref[0]
    comps, planes, reach, members, depth = sources[0].shape
    width = reach - 2
    half = width // 2
    count = groups * members
    wide = 2 * depth

    @pl.loop(0, comps)
    def _(c):
        for g in range(2):
            first = g * half
            lhs = jnp.concatenate(
                [
                    jnp.concatenate(
                        [piece for p in range(planes) for piece in three_rows(source.at[c, p], first, half)], axis=1
                    )
                    for source in sources
                ],
                axis=0,
            )
            both = jnp.dot(lhs, weights_ref[...], preferred_element_type=jnp.float32)
            edge_ref[c, g] = both[:, g * wide : (g + 1) * wide]
            beside = weights_ref[3 * depth : 6 * depth, :wide]
            cross_ref[c, g] = jnp.dot(
                lhs[:, 3 * g * depth : 3 * (g + 1) * depth], beside, preferred_element_type=jnp.float32
            )
            inner = both[:, (1 - g) * wide : (2 - g) * wide]
            for y in range(half):
                label = labels_ref[1 - g, pl.ds(me * width + first + y, 1), :]
                density = density_at(label, density_ref, materials)
                near = pl.ds(pl.multiple_of(((c * 2 + g) * half + y) * depth, depth), depth)
                edge = pl.ds(pl.multiple_of((c * half + y) * depth, depth), depth)
                for m in range(groups):
                    start = pl.multiple_of((me ^ m) * members, members)
                    near_left[pl.ds(start, members), near] = sources[m][c, 1 - g, first + y + 1]
                    left_ref[g, pl.ds(start, members), edge] = sources[m][c, g, first + y + 1]
                    at = (m * half + y) * members
                    put_images(
                        inner[at : at + members], label, density, near_right, start, near, count, materials
                    )

    part_ref[...] = correlate(near_left[...], near_right[...])


def vmem_spec():
    return pl.BlockSpec(memory_space=pltpu.VMEM)


def smem_spec():
    return pl.BlockSpec(memory_space=pltpu.SMEM)


def pack_kernel(pairs, me_ref, *refs):
    blocks, up_ref, down_ref = refs[:pairs], refs[-2], refs[-1]
    comps, planes, reach, members, depth = blocks[0].shape
    half = (reach - 2) // 2
    for i, block in enumerate(blocks):
        for c in range(comps):
            up_ref[i * comps + c] = block[c, planes - 1, 0 : half + 2]
            down_ref[i * comps + c] = block[c, 0, half : 2 * half + 2]
    if up_ref.shape[0] > pairs * comps:
        labels_ref = refs[pairs]
        for out, plane, first in ((up_ref, planes - 1, 0), (down_ref, 0, half)):
            for y in range(half + 2):
                row = labels_ref[plane, pl.ds(me_ref[0] * 2 * half + first + min(y, half - 1), 1), :]
                out[pairs * comps, y] = jnp.broadcast_to(row, (members, depth)).astype(jnp.float32).astype(out.dtype)


def pack(pair, labels, me):
    comps, planes, reach, members, depth = pair[0].shape
    extra = [] if labels is None else [labels]
    out = jax.ShapeDtypeStruct(
        (len(pair) * comps + len(extra), (reach - 2) // 2 + 2, members, depth), pair[0].dtype
    )
    return pl.pallas_call(
        functools.partial(pack_kernel, len(pair)),
        out_shape=[out, out],
        in_specs=[smem_spec()] + [vmem_spec()] * (len(pair) + len(extra)),
        out_specs=[vmem_spec()] * 2,
        compiler_params=pltpu.CompilerParams(vmem_limit_bytes=16 * 2**20),
        cost_estimate=pl.CostEstimate(flops=0, bytes_accessed=2**20, transcendentals=0),
    )(me, *pair, *extra)


def local_tiles(blocks, labels, density, me):
    groups = len(blocks)
    comps, planes, reach, members, depth = blocks[0].shape
    half = (reach - 2) // 2
    count = groups * members
    columns = (density.shape[0] + 1) * count
    same, beside = stencil_weights(depth)
    weights = jnp.asarray(
        np.concatenate([np.concatenate([same, beside], axis=0), np.concatenate([beside, same], axis=0)], axis=1),
        jnp.bfloat16,
    )
    image = jax.ShapeDtypeStruct((comps, 2, groups * half * members, 2 * depth), jnp.float32)
    return pl.pallas_call(
        functools.partial(local_kernel, groups, density.shape[0]),
        out_shape=[
            jax.ShapeDtypeStruct((count, columns), jnp.float32),
            image,
            image,
            jax.ShapeDtypeStruct((2, count, comps * half * depth), jnp.bfloat16),
        ],
        in_specs=[smem_spec(), smem_spec()] + [vmem_spec()] * (groups + 2),
        out_specs=[vmem_spec()] * 4,
        scratch_shapes=[
            pltpu.VMEM((count, comps * 2 * half * depth), jnp.bfloat16),
            pltpu.VMEM((columns, comps * 2 * half * depth), jnp.bfloat16),
        ],
        compiler_params=pltpu.CompilerParams(vmem_limit_bytes=40 * 2**20),
        cost_estimate=pl.CostEstimate(flops=5 * 10**9, bytes_accessed=12 * 2**20, transcendentals=0),
    )(me, density, *blocks, labels, weights)


def received_at(side, m, groups, comps, c):
    each = groups // len(side)
    return side[m // each].at[(m % each) * comps + c]


def returns_kernel(groups, materials, pairs, me_ref, density_ref, cross_ref, *refs):
    sides = (refs[:pairs], refs[pairs : 2 * pairs])
    below_ref, above_ref, left, right = refs[2 * pairs :]
    me = me_ref[0]
    comps = cross_ref.shape[0]
    reach, members, depth = sides[0][0].shape[1:]
    half = reach - 2
    count = groups * members

    @pl.loop(0, comps)
    def _(c):
        for g in range(2):
            cross = cross_ref[c, g]
            for y in range(half):
                label = sides[g][0][(groups // pairs) * comps, y].astype(jnp.float32)
                density = density_at(label, density_ref, materials)
                lanes = pl.ds(pl.multiple_of((c * half + y) * depth, depth), depth)
                for m in range(groups):
                    start = pl.multiple_of((me ^ m) * members, members)
                    left[g, pl.ds(start, members), lanes] = received_at(sides[g], m, groups, comps, c)[y + 1]
                    at = (m * half + y) * members
                    put_images(
                        cross[at : at + members], label, density, right.at[g], start, lanes, count, materials
                    )

    below_ref[...] = correlate(left[0], right[0])
    above_ref[...] = correlate(left[1], right[1])


def return_tiles(cross, lows, highs, density, me, groups):
    materials = density.shape[0]
    comps = cross.shape[0]
    reach, members, depth = lows[0].shape[1:]
    count = groups * members
    cells = comps * (reach - 2) * depth
    columns = (materials + 1) * count
    part = jax.ShapeDtypeStruct((count, columns), jnp.float32)
    halos = [*lows, *highs]
    return pl.pallas_call(
        functools.partial(returns_kernel, groups, materials, len(lows)),
        out_shape=[part, part],
        in_specs=[smem_spec(), smem_spec()] + [vmem_spec()] * (1 + len(halos)),
        out_specs=[vmem_spec()] * 2,
        scratch_shapes=[
            pltpu.VMEM((2, count, cells), jnp.bfloat16),
            pltpu.VMEM((2, columns, cells), jnp.bfloat16),
        ],
        compiler_params=pltpu.CompilerParams(vmem_limit_bytes=40 * 2**20),
        cost_estimate=pl.CostEstimate(flops=3 * 10**9, bytes_accessed=6 * 2**20, transcendentals=0),
    )(me, density, cross, *halos)


def edge_kernel(groups, materials, pairs, me_ref, density_ref, near_ref, edge_ref, left_ref, *refs):
    sides = (refs[:pairs], refs[pairs : 2 * pairs])
    labels_ref, weights_ref, part_ref, right = refs[2 * pairs :]
    me = me_ref[0]
    comps = edge_ref.shape[0]
    reach, members, depth = sides[0][0].shape[1:]
    half = reach - 2
    width = 2 * half
    count = groups * members

    @pl.loop(0, comps)
    def _(c):
        for g in range(2):
            lhs = jnp.concatenate(
                [
                    jnp.concatenate(three_rows(received_at(sides[g], m, groups, comps, c), 0, half), axis=1)
                    for m in range(groups)
                ],
                axis=0,
            )
            image = edge_ref[c, g] + jnp.dot(lhs, weights_ref[...], preferred_element_type=jnp.float32)
            for y in range(half):
                label = labels_ref[g, pl.ds(me * width + g * half + y, 1), :]
                density = density_at(label, density_ref, materials)
                lanes = pl.ds(pl.multiple_of((c * half + y) * depth, depth), depth)
                for m in range(groups):
                    start = pl.multiple_of((me ^ m) * members, members)
                    at = (m * half + y) * members
                    put_images(
                        image[at : at + members], label, density, right.at[g], start, lanes, count, materials
                    )

    part_ref[...] = near_ref[...] + correlate(left_ref[0], right[0]) + correlate(left_ref[1], right[1])


def combine_kernel(part_ref, below_ref, above_ref, from_below_ref, from_above_ref, slab_ref, wide_ref):
    count = part_ref.shape[0]
    copies = wide_ref.shape[0] // count
    part = part_ref[...]
    slab_ref[...] = part + (from_below_ref[...] + from_above_ref[...])
    total = part + (below_ref[...] + above_ref[...])
    for s in range(count):
        for r in range(copies):
            wide_ref[s * copies + r] = total[s : s + 1]


def combine(part, returns, copies):
    count, columns = part.shape
    return pl.pallas_call(
        combine_kernel,
        out_shape=[
            jax.ShapeDtypeStruct((count, columns), jnp.float32),
            jax.ShapeDtypeStruct((count * copies, 1, columns), jnp.float32),
        ],
        in_specs=[vmem_spec()] * (1 + len(returns)),
        out_specs=[vmem_spec()] * 2,
        compiler_params=pltpu.CompilerParams(vmem_limit_bytes=16 * 2**20),
        cost_estimate=pl.CostEstimate(flops=0, bytes_accessed=2**19, transcendentals=0),
    )(part, *returns)


def edge_tiles(near, edge, left, lows, highs, labels, density, me, groups):
    count, columns = near.shape
    materials = density.shape[0]
    weights = jnp.asarray(stencil_weights(labels.shape[2])[1], jnp.bfloat16)
    part = jax.ShapeDtypeStruct((count, columns), jnp.float32)
    halos = [*lows, *highs]
    return pl.pallas_call(
        functools.partial(edge_kernel, groups, materials, len(lows)),
        out_shape=part,
        in_specs=[smem_spec(), smem_spec()] + [vmem_spec()] * (5 + len(halos)),
        out_specs=vmem_spec(),
        scratch_shapes=[pltpu.VMEM((2, columns, left.shape[2]), jnp.bfloat16)],
        compiler_params=pltpu.CompilerParams(vmem_limit_bytes=40 * 2**20),
        cost_estimate=pl.CostEstimate(flops=5 * 10**9, bytes_accessed=20 * 2**20, transcendentals=0),
    )(me, density, near, edge, left, *halos, labels, weights)


def finish_kernel(count, slab_scale, gram_scale, *refs):
    parts, rows_ref, slab_ref, gram_ref = refs[:-3], refs[-3], refs[-2], refs[-1]
    terms = [p[...] for p in parts]
    while len(terms) > 1:
        terms = [terms[i] + terms[i + 1] for i in range(0, len(terms), 2)]
    slab = terms[0] * slab_scale
    gram = jnp.sum(rows_ref[...], axis=0) * gram_scale
    for j in range(slab.shape[1] // count):
        slab_ref[0, j] = slab[:, j * count : (j + 1) * count]
        gram_ref[j] = gram[:, j * count : (j + 1) * count]


def finish(parts, rows, slab_scale, gram_scale):
    count, columns = parts[0].shape
    blocks = columns // count
    return pl.pallas_call(
        functools.partial(finish_kernel, count, slab_scale, gram_scale),
        out_shape=[
            jax.ShapeDtypeStruct((1, blocks, count, count), jnp.float32),
            jax.ShapeDtypeStruct((blocks, 1, count), jnp.float32),
        ],
        in_specs=[vmem_spec()] * (1 + len(parts)),
        out_specs=[vmem_spec()] * 2,
        compiler_params=pltpu.CompilerParams(vmem_limit_bytes=16 * 2**20),
    )(*parts, rows)


def body(snapshots, labels, free_mask, density):
    groups, slabs = lax.axis_size("snap"), lax.axis_size("space")
    planes, rows, depth = labels.shape
    me = lax.axis_index("snap").astype(jnp.int32).reshape(1)
    with jax.named_scope("spread"):
        mine = spread(snapshots, free_mask, me, groups)
    with jax.named_scope("regroup"):
        blocks = [mine[0]] + [
            lax.ppermute(mine[m], "snap", [(i, i ^ m) for i in range(groups)]) for m in range(1, groups)
        ]
    with jax.named_scope("halo"):
        forward = [(i, i + 1) for i in range(slabs - 1)]
        backward = [(b, a) for a, b in forward]
        lows, highs = [], []
        for start in range(0, groups, 2):
            pair = blocks[start : start + 2]
            if lows:
                pair, *_ = lax.optimization_barrier((pair, sent_up, sent_down))
            sent_up, sent_down = pack(pair, None if lows else labels, me)
            if not lows:
                pair, sent_up, sent_down = lax.optimization_barrier((pair, sent_up, sent_down))
            lows.append(lax.ppermute(sent_up, "space", forward))
            highs.append(lax.ppermute(sent_down, "space", backward))
    with jax.named_scope("local_tiles"):
        near, edge, cross, left = local_tiles(blocks, labels, density, me)
    with jax.named_scope("return_tiles"):
        below, above = return_tiles(cross, lows, highs, density, me, groups)
        from_above = lax.ppermute(below, "space", backward)
        from_below = lax.ppermute(above, "space", forward)
    with jax.named_scope("edge_tiles"):
        part = edge_tiles(near, edge, left, lows, highs, labels, density, me, groups)
    with jax.named_scope("sums"):
        part, wide = combine(part, (below, above, from_below, from_above), groups)
        sent = lax.all_to_all(wide, ("space", "snap"), 0, 0, tiled=True)
        parts = [part] + [
            lax.ppermute(part, "snap", [(i, i ^ m) for i in range(groups)]) for m in range(1, groups)
        ]
        slab_scale = 1.0 / (3.0 * planes * rows * depth)
        slab, gram = finish(parts, sent, slab_scale, slab_scale / slabs)
    return gram, slab


def solution(mesh):
    in_specs = (
        P("snap", None, "space", None, None),
        P("space", None, None),
        P("space", None, None),
        P(),
    )
    out_specs = (P(None, "space", None), P("space", None, None, None))
    return jax.shard_map(body, mesh=mesh, in_specs=in_specs, out_specs=out_specs, check_vma=False)
```

```python
import functools

import jax
import jax.numpy as jnp
import numpy as np
from jax import lax
from jax.experimental import pallas as pl
from jax.experimental.pallas import tpu as pltpu
from jax.sharding import PartitionSpec as P


def spread_kernel(groups, width, me_ref, snaps_ref, mask_ref, *refs):
    outs, turned = refs[:groups], refs[groups]
    rows = snaps_ref.shape[3]
    me = me_ref[0]
    mask = mask_ref[0].astype(jnp.float32)
    values = snaps_ref[:, 0, 0].astype(jnp.float32) * mask[None]
    edge = jnp.zeros(turned.shape[1:], turned.dtype)
    turned[0] = edge
    turned[rows + 1] = edge
    turned[1 : rows + 1] = jnp.swapaxes(values, 0, 1).astype(turned.dtype)
    for m in range(groups):
        outs[m][0, 0] = turned[pl.ds((me ^ m) * width, width + 2)]


def spread(snapshots, free_mask, me, groups):
    members, comps, planes, rows, depth = snapshots.shape
    width = rows // groups
    block = jax.ShapeDtypeStruct((comps, planes, width + 2, members, depth), snapshots.dtype)
    out_spec = pl.BlockSpec((1, 1, width + 2, members, depth), lambda c, p, me: (c, p, 0, 0, 0))
    return pl.pallas_call(
        functools.partial(spread_kernel, groups, width),
        out_shape=[block] * groups,
        grid_spec=pltpu.PrefetchScalarGridSpec(
            num_scalar_prefetch=1,
            grid=(comps, planes),
            in_specs=[
                pl.BlockSpec((members, 1, 1, rows, depth), lambda c, p, me: (0, c, p, 0, 0)),
                pl.BlockSpec((1, rows, depth), lambda c, p, me: (p, 0, 0)),
            ],
            out_specs=[out_spec] * groups,
            scratch_shapes=[pltpu.VMEM((rows + 2, members, depth), snapshots.dtype)],
        ),
        compiler_params=pltpu.CompilerParams(vmem_limit_bytes=32 * 2**20),
        cost_estimate=pl.CostEstimate(flops=0, bytes_accessed=5 * 2**20, transcendentals=0),
    )(me, snapshots, free_mask)


def stencil_weights(depth):
    mass = {-1: 1.0, 0: 4.0, 1: 1.0}
    stiff = {-1: -1.0, 0: 2.0, 1: -1.0}
    near = np.eye(depth, k=1) + np.eye(depth, k=-1)
    mass_z = 4.0 * np.eye(depth) + near
    stiff_z = 2.0 * np.eye(depth) - near

    def plane(dx):
        blocks = []
        for dy in (-1, 0, 1):
            both = mass[dx] * mass[dy]
            mixed = stiff[dx] * mass[dy] + mass[dx] * stiff[dy]
            blocks.append(np.concatenate([both * mass_z, mixed * mass_z + both * stiff_z], axis=1))
        return np.concatenate(blocks, axis=0)

    return plane(0), plane(1)


def three_rows(block, first, height):
    members, depth = block.shape[-2:]
    return [block[first + dy : first + dy + height].reshape(height * members, depth) for dy in range(3)]


def density_at(label, density_ref, materials):
    density = jnp.zeros(label.shape, jnp.float32)
    for j in range(materials):
        density = density + jnp.where(label == j, density_ref[j] * (1.0 / 216.0), 0.0)
    return density


def put_images(image, label, density, right, start, lanes, count, materials):
    members, depth = image.shape[0], image.shape[1] // 2
    right[pl.ds(start, members), lanes] = (image[:, :depth] * density).astype(right.dtype)
    stiff = image[:, depth:] * (1.0 / 36.0)
    for j in range(materials):
        at = pl.multiple_of((j + 1) * count + start, members)
        right[pl.ds(at, members), lanes] = jnp.where(label == j, stiff, 0.0).astype(right.dtype)


def correlate(left, right):
    return lax.dot_general(left, right, (((1,), (1,)), ((), ())), preferred_element_type=jnp.float32)


def local_kernel(groups, materials, me_ref, density_ref, *refs):
    sources = refs[:groups]
    labels_ref, weights_ref, part_ref, edge_ref, cross_ref, left_ref, near_left, near_right = refs[groups:]
    me = me_ref[0]
    comps, planes, reach, members, depth = sources[0].shape
    width = reach - 2
    half = width // 2
    count = groups * members
    wide = 2 * depth

    @pl.loop(0, comps)
    def _(c):
        for g in range(2):
            first = g * half
            lhs = jnp.concatenate(
                [
                    jnp.concatenate(
                        [piece for p in range(planes) for piece in three_rows(source.at[c, p], first, half)], axis=1
                    )
                    for source in sources
                ],
                axis=0,
            )
            both = jnp.dot(lhs, weights_ref[...], preferred_element_type=jnp.float32)
            edge_ref[c, g] = both[:, g * wide : (g + 1) * wide]
            beside = weights_ref[3 * depth : 6 * depth, :wide]
            cross_ref[c, g] = jnp.dot(
                lhs[:, 3 * g * depth : 3 * (g + 1) * depth], beside, preferred_element_type=jnp.float32
            )
            inner = both[:, (1 - g) * wide : (2 - g) * wide]
            for y in range(half):
                label = labels_ref[1 - g, pl.ds(me * width + first + y, 1), :]
                density = density_at(label, density_ref, materials)
                near = pl.ds(pl.multiple_of(((c * 2 + g) * half + y) * depth, depth), depth)
                edge = pl.ds(pl.multiple_of((c * half + y) * depth, depth), depth)
                for m in range(groups):
                    start = pl.multiple_of((me ^ m) * members, members)
                    near_left[pl.ds(start, members), near] = sources[m][c, 1 - g, first + y + 1]
                    left_ref[g, pl.ds(start, members), edge] = sources[m][c, g, first + y + 1]
                    at = (m * half + y) * members
                    put_images(
                        inner[at : at + members], label, density, near_right, start, near, count, materials
                    )

    part_ref[...] = correlate(near_left[...], near_right[...])


def vmem_spec():
    return pl.BlockSpec(memory_space=pltpu.VMEM)


def smem_spec():
    return pl.BlockSpec(memory_space=pltpu.SMEM)


def pack_kernel(pairs, me_ref, *refs):
    blocks, outs = refs[:pairs], refs[-2:]
    comps, planes, reach, members, depth = blocks[0].shape
    half = (reach - 2) // 2
    for out, up in ((outs[0], 1 - me_ref[1]), (outs[1], me_ref[1])):
        first = (1 - up) * half
        for i, block in enumerate(blocks):
            for c in range(comps):
                out[i * comps + c] = block[c, up * (planes - 1), pl.ds(first, half + 2)]
        if out.shape[0] > pairs * comps:
            labels_ref = refs[pairs]
            for y in range(half + 2):
                at = me_ref[0] * 2 * half + first + min(y, half - 1)
                row = labels_ref[up * (planes - 1), pl.ds(at, 1), :]
                out[pairs * comps, y] = jnp.broadcast_to(row, (members, depth)).astype(jnp.float32).astype(out.dtype)


def pack(pair, labels, me):
    comps, planes, reach, members, depth = pair[0].shape
    extra = [] if labels is None else [labels]
    out = jax.ShapeDtypeStruct(
        (len(pair) * comps + len(extra), (reach - 2) // 2 + 2, members, depth), pair[0].dtype
    )
    return pl.pallas_call(
        functools.partial(pack_kernel, len(pair)),
        out_shape=[out, out],
        in_specs=[smem_spec()] + [vmem_spec()] * (len(pair) + len(extra)),
        out_specs=[vmem_spec()] * 2,
        compiler_params=pltpu.CompilerParams(vmem_limit_bytes=16 * 2**20),
        cost_estimate=pl.CostEstimate(flops=0, bytes_accessed=2**20, transcendentals=0),
    )(me, *pair, *extra)


def local_tiles(blocks, labels, density, me):
    groups = len(blocks)
    comps, planes, reach, members, depth = blocks[0].shape
    half = (reach - 2) // 2
    count = groups * members
    columns = (density.shape[0] + 1) * count
    same, beside = stencil_weights(depth)
    weights = jnp.asarray(
        np.concatenate([np.concatenate([same, beside], axis=0), np.concatenate([beside, same], axis=0)], axis=1),
        jnp.bfloat16,
    )
    image = jax.ShapeDtypeStruct((comps, 2, groups * half * members, 2 * depth), jnp.float32)
    return pl.pallas_call(
        functools.partial(local_kernel, groups, density.shape[0]),
        out_shape=[
            jax.ShapeDtypeStruct((count, columns), jnp.float32),
            image,
            image,
            jax.ShapeDtypeStruct((2, count, comps * half * depth), jnp.bfloat16),
        ],
        in_specs=[smem_spec(), smem_spec()] + [vmem_spec()] * (groups + 2),
        out_specs=[vmem_spec()] * 4,
        scratch_shapes=[
            pltpu.VMEM((count, comps * 2 * half * depth), jnp.bfloat16),
            pltpu.VMEM((columns, comps * 2 * half * depth), jnp.bfloat16),
        ],
        compiler_params=pltpu.CompilerParams(vmem_limit_bytes=40 * 2**20),
        cost_estimate=pl.CostEstimate(flops=5 * 10**9, bytes_accessed=12 * 2**20, transcendentals=0),
    )(me, density, *blocks, labels, weights)


def received_at(side, m, comps, c):
    part = 0
    while m >= side[part].shape[0] // comps:
        m -= side[part].shape[0] // comps
        part += 1
    return side[part].at[m * comps + c]


def returns_kernel(groups, materials, pairs, me_ref, density_ref, cross_ref, *refs):
    sides = (refs[:pairs], refs[pairs : 2 * pairs])
    below_ref, above_ref, left, right = refs[2 * pairs :]
    me = me_ref[0]
    comps = cross_ref.shape[0]
    reach, members, depth = sides[0][0].shape[1:]
    half = reach - 2
    count = groups * members

    @pl.loop(0, comps)
    def _(c):
        for side in range(2):
            g = me_ref[1] if side else 1 - me_ref[1]
            cross = cross_ref[c, g]
            for y in range(half):
                label = sides[side][0][sides[side][0].shape[0] - 1, y].astype(jnp.float32)
                density = density_at(label, density_ref, materials)
                lanes = pl.ds(pl.multiple_of((c * half + y) * depth, depth), depth)
                for m in range(groups):
                    start = pl.multiple_of((me ^ m) * members, members)
                    left[side, pl.ds(start, members), lanes] = received_at(sides[side], m, comps, c)[y + 1]
                    at = (m * half + y) * members
                    put_images(
                        cross[at : at + members], label, density, right.at[side], start, lanes, count, materials
                    )

    below_ref[...] = correlate(left[0], right[0])
    above_ref[...] = correlate(left[1], right[1])


def return_tiles(cross, lows, highs, density, me, groups):
    materials = density.shape[0]
    comps = cross.shape[0]
    reach, members, depth = lows[0].shape[1:]
    count = groups * members
    cells = comps * (reach - 2) * depth
    columns = (materials + 1) * count
    part = jax.ShapeDtypeStruct((count, columns), jnp.float32)
    halos = [*lows, *highs]
    return pl.pallas_call(
        functools.partial(returns_kernel, groups, materials, len(lows)),
        out_shape=[part, part],
        in_specs=[smem_spec(), smem_spec()] + [vmem_spec()] * (1 + len(halos)),
        out_specs=[vmem_spec()] * 2,
        scratch_shapes=[
            pltpu.VMEM((2, count, cells), jnp.bfloat16),
            pltpu.VMEM((2, columns, cells), jnp.bfloat16),
        ],
        compiler_params=pltpu.CompilerParams(vmem_limit_bytes=40 * 2**20),
        cost_estimate=pl.CostEstimate(flops=3 * 10**9, bytes_accessed=6 * 2**20, transcendentals=0),
    )(me, density, cross, *halos)


def edge_kernel(groups, materials, pairs, me_ref, density_ref, near_ref, edge_ref, left_ref, *refs):
    sides = (refs[:pairs], refs[pairs : 2 * pairs])
    labels_ref, weights_ref, part_ref, right = refs[2 * pairs :]
    me = me_ref[0]
    comps = edge_ref.shape[0]
    reach, members, depth = sides[0][0].shape[1:]
    half = reach - 2
    width = 2 * half
    count = groups * members

    @pl.loop(0, comps)
    def _(c):
        for side in range(2):
            g = me_ref[1] if side else 1 - me_ref[1]
            lhs = jnp.concatenate(
                [
                    jnp.concatenate(three_rows(received_at(sides[side], m, comps, c), 0, half), axis=1)
                    for m in range(groups)
                ],
                axis=0,
            )
            image = edge_ref[c, g] + jnp.dot(lhs, weights_ref[...], preferred_element_type=jnp.float32)
            for y in range(half):
                label = labels_ref[g, pl.ds(me * width + g * half + y, 1), :]
                density = density_at(label, density_ref, materials)
                lanes = pl.ds(pl.multiple_of((c * half + y) * depth, depth), depth)
                for m in range(groups):
                    start = pl.multiple_of((me ^ m) * members, members)
                    at = (m * half + y) * members
                    put_images(
                        image[at : at + members], label, density, right.at[g], start, lanes, count, materials
                    )

    part_ref[...] = near_ref[...] + correlate(left_ref[0], right[0]) + correlate(left_ref[1], right[1])


def combine_kernel(part_ref, below_ref, above_ref, from_below_ref, from_above_ref, slab_ref, wide_ref):
    count = part_ref.shape[0]
    copies = wide_ref.shape[0] // count
    part = part_ref[...]
    slab_ref[...] = part + (from_below_ref[...] + from_above_ref[...])
    total = part + (below_ref[...] + above_ref[...])
    for s in range(count):
        for r in range(copies):
            wide_ref[s * copies + r] = total[s : s + 1]


def combine(part, returns, copies):
    count, columns = part.shape
    return pl.pallas_call(
        combine_kernel,
        out_shape=[
            jax.ShapeDtypeStruct((count, columns), jnp.float32),
            jax.ShapeDtypeStruct((count * copies, 1, columns), jnp.float32),
        ],
        in_specs=[vmem_spec()] * (1 + len(returns)),
        out_specs=[vmem_spec()] * 2,
        compiler_params=pltpu.CompilerParams(vmem_limit_bytes=16 * 2**20),
        cost_estimate=pl.CostEstimate(flops=0, bytes_accessed=2**19, transcendentals=0),
    )(part, *returns)


def edge_tiles(near, edge, left, lows, highs, labels, density, me, groups):
    count, columns = near.shape
    materials = density.shape[0]
    weights = jnp.asarray(stencil_weights(labels.shape[2])[1], jnp.bfloat16)
    part = jax.ShapeDtypeStruct((count, columns), jnp.float32)
    halos = [*lows, *highs]
    return pl.pallas_call(
        functools.partial(edge_kernel, groups, materials, len(lows)),
        out_shape=part,
        in_specs=[smem_spec(), smem_spec()] + [vmem_spec()] * (5 + len(halos)),
        out_specs=vmem_spec(),
        scratch_shapes=[pltpu.VMEM((2, columns, left.shape[2]), jnp.bfloat16)],
        compiler_params=pltpu.CompilerParams(vmem_limit_bytes=40 * 2**20),
        cost_estimate=pl.CostEstimate(flops=5 * 10**9, bytes_accessed=20 * 2**20, transcendentals=0),
    )(me, density, near, edge, left, *halos, labels, weights)


def finish_kernel(count, slab_scale, gram_scale, *refs):
    parts, rows_ref, slab_ref, gram_ref = refs[:-3], refs[-3], refs[-2], refs[-1]
    terms = [p[...] for p in parts]
    while len(terms) > 1:
        terms = [terms[i] + terms[i + 1] for i in range(0, len(terms), 2)]
    slab = terms[0] * slab_scale
    gram = jnp.sum(rows_ref[...], axis=0) * gram_scale
    for j in range(slab.shape[1] // count):
        slab_ref[0, j] = slab[:, j * count : (j + 1) * count]
        gram_ref[j] = gram[:, j * count : (j + 1) * count]


def finish(parts, rows, slab_scale, gram_scale):
    count, columns = parts[0].shape
    blocks = columns // count
    return pl.pallas_call(
        functools.partial(finish_kernel, count, slab_scale, gram_scale),
        out_shape=[
            jax.ShapeDtypeStruct((1, blocks, count, count), jnp.float32),
            jax.ShapeDtypeStruct((blocks, 1, count), jnp.float32),
        ],
        in_specs=[vmem_spec()] * (1 + len(parts)),
        out_specs=[vmem_spec()] * 2,
        compiler_params=pltpu.CompilerParams(vmem_limit_bytes=16 * 2**20),
    )(*parts, rows)


def body(snapshots, labels, free_mask, density):
    groups, slabs = lax.axis_size("snap"), lax.axis_size("space")
    planes, rows, depth = labels.shape
    me = jnp.stack([lax.axis_index("snap"), lax.axis_index("space") % 2]).astype(jnp.int32)
    with jax.named_scope("spread"):
        mine = spread(snapshots, free_mask, lax.axis_index("snap").astype(jnp.int32).reshape(1), groups)
    with jax.named_scope("regroup"):
        blocks = [mine[0]] + [
            lax.ppermute(mine[m], "snap", [(i, i ^ m) for i in range(groups)]) for m in range(1, groups)
        ]
    with jax.named_scope("halo"):
        even = [(i, i ^ 1) for i in range(slabs)]
        odd = [(i, ((i + 1) ^ 1) - 1) for i in range(1, slabs - 1)]
        firsts, seconds = [], []
        for start in range(0, groups, 2):
            some = blocks[start : start + 2]
            if firsts:
                some, *_ = lax.optimization_barrier((some, to_even, to_odd))
            to_even, to_odd = pack(some, None if firsts else labels, me)
            if not firsts:
                some, to_even, to_odd = lax.optimization_barrier((some, to_even, to_odd))
            seconds.append(lax.ppermute(to_odd, "space", odd))
            firsts.append(lax.ppermute(to_even, "space", even))
    with jax.named_scope("local_tiles"):
        near, edge, cross, left = local_tiles(blocks, labels, density, me)
    with jax.named_scope("return_tiles"):
        below, above = return_tiles(cross, firsts, seconds, density, me, groups)
        from_below = lax.ppermute(below, "space", even)
        from_above = lax.ppermute(above, "space", odd)
    with jax.named_scope("edge_tiles"):
        part = edge_tiles(near, edge, left, firsts, seconds, labels, density, me, groups)
    with jax.named_scope("sums"):
        part, wide = combine(part, (below, above, from_below, from_above), groups)
        sent = lax.all_to_all(wide, ("space", "snap"), 0, 0, tiled=True)
        parts = [part] + [
            lax.ppermute(part, "snap", [(i, i ^ m) for i in range(groups)]) for m in range(1, groups)
        ]
        slab_scale = 1.0 / (3.0 * planes * rows * depth)
        slab, gram = finish(parts, sent, slab_scale, slab_scale / slabs)
    return gram, slab


def solution(mesh):
    in_specs = (
        P("snap", None, "space", None, None),
        P("space", None, None),
        P("space", None, None),
        P(),
    )
    out_specs = (P(None, "space", None), P("space", None, None, None))
    return jax.shard_map(body, mesh=mesh, in_specs=in_specs, out_specs=out_specs, check_vma=False)
```

```python
import functools

import jax
import jax.numpy as jnp
import numpy as np
from jax import lax
from jax.experimental import pallas as pl
from jax.experimental.pallas import tpu as pltpu
from jax.sharding import PartitionSpec as P


def spread_kernel(groups, width, me_ref, snaps_ref, mask_ref, *refs):
    outs, turned = refs[:groups], refs[groups]
    rows = snaps_ref.shape[3]
    me = me_ref[0]
    mask = mask_ref[0].astype(jnp.float32)
    values = snaps_ref[:, 0, 0].astype(jnp.float32) * mask[None]
    edge = jnp.zeros(turned.shape[1:], turned.dtype)
    turned[0] = edge
    turned[rows + 1] = edge
    turned[1 : rows + 1] = jnp.swapaxes(values, 0, 1).astype(turned.dtype)
    for m in range(groups):
        outs[m][0, 0] = turned[pl.ds((me ^ m) * width, width + 2)]


def spread(snapshots, free_mask, me, groups):
    members, comps, planes, rows, depth = snapshots.shape
    width = rows // groups
    block = jax.ShapeDtypeStruct((comps, planes, width + 2, members, depth), snapshots.dtype)
    out_spec = pl.BlockSpec((1, 1, width + 2, members, depth), lambda c, p, me: (c, p, 0, 0, 0))
    return pl.pallas_call(
        functools.partial(spread_kernel, groups, width),
        out_shape=[block] * groups,
        grid_spec=pltpu.PrefetchScalarGridSpec(
            num_scalar_prefetch=1,
            grid=(comps, planes),
            in_specs=[
                pl.BlockSpec((members, 1, 1, rows, depth), lambda c, p, me: (0, c, p, 0, 0)),
                pl.BlockSpec((1, rows, depth), lambda c, p, me: (p, 0, 0)),
            ],
            out_specs=[out_spec] * groups,
            scratch_shapes=[pltpu.VMEM((rows + 2, members, depth), snapshots.dtype)],
        ),
        compiler_params=pltpu.CompilerParams(vmem_limit_bytes=32 * 2**20),
        cost_estimate=pl.CostEstimate(flops=0, bytes_accessed=5 * 2**20, transcendentals=0),
    )(me, snapshots, free_mask)


def put_stencil(weights_ref, planes):
    depth = weights_ref.shape[1] // (2 * planes)
    apart = jnp.abs(
        lax.broadcasted_iota(jnp.int32, (depth, depth), 0) - lax.broadcasted_iota(jnp.int32, (depth, depth), 1)
    )
    mass, stiff = (4.0, 1.0), (2.0, -1.0)
    for q in range(planes):
        for dy in range(3):
            for p in range(planes):
                x, y = abs(q - p), abs(dy - 1)
                both = mass[x] * mass[y]
                mixed = stiff[x] * mass[y] + mass[x] * stiff[y]
                for kind, (same, beside) in enumerate(
                    ((4.0 * both, both), (4.0 * mixed + 2.0 * both, mixed - both))
                ):
                    block = jnp.where(apart == 0, same, jnp.where(apart == 1, beside, 0.0))
                    weights_ref[
                        (q * 3 + dy) * depth : (q * 3 + dy + 1) * depth,
                        (p * 2 + kind) * depth : (p * 2 + kind + 1) * depth,
                    ] = block.astype(weights_ref.dtype)


def three_rows(block, first, height):
    members, depth = block.shape[-2:]
    return [block[first + dy : first + dy + height].reshape(height * members, depth) for dy in range(3)]


def density_at(label, density_ref, materials):
    density = jnp.zeros(label.shape, jnp.float32)
    for j in range(materials):
        density = density + jnp.where(label == j, density_ref[j] * (1.0 / 216.0), 0.0)
    return density


def put_images(image, label, density, right, start, lanes, count, materials):
    members, depth = image.shape[0], image.shape[1] // 2
    right[pl.ds(start, members), lanes] = (image[:, :depth] * density).astype(right.dtype)
    stiff = image[:, depth:] * (1.0 / 36.0)
    for j in range(materials):
        at = pl.multiple_of((j + 1) * count + start, members)
        right[pl.ds(at, members), lanes] = jnp.where(label == j, stiff, 0.0).astype(right.dtype)


def correlate(left, right):
    return lax.dot_general(left, right, (((1,), (1,)), ((), ())), preferred_element_type=jnp.float32)


def local_kernel(groups, materials, me_ref, density_ref, *refs):
    sources = refs[:groups]
    labels_ref, weights_ref, part_ref, edge_ref, cross_ref, left_ref, near_left, near_right = refs[groups:]
    me = me_ref[0]
    comps, planes, reach, members, depth = sources[0].shape
    width = reach - 2
    half = width // 2
    count = groups * members
    wide = 2 * depth

    @pl.loop(0, comps)
    def _(c):
        for g in range(2):
            first = g * half
            lhs = jnp.concatenate(
                [
                    jnp.concatenate(
                        [piece for p in range(planes) for piece in three_rows(source.at[c, p], first, half)], axis=1
                    )
                    for source in sources
                ],
                axis=0,
            )
            both = jnp.dot(lhs, weights_ref[...], preferred_element_type=jnp.float32)
            edge_ref[c, g] = both[:, g * wide : (g + 1) * wide]
            beside = weights_ref[3 * depth : 6 * depth, :wide]
            cross_ref[c, g] = jnp.dot(
                lhs[:, 3 * g * depth : 3 * (g + 1) * depth], beside, preferred_element_type=jnp.float32
            )
            inner = both[:, (1 - g) * wide : (2 - g) * wide]
            for y in range(half):
                label = labels_ref[1 - g, pl.ds(me * width + first + y, 1), :]
                density = density_at(label, density_ref, materials)
                near = pl.ds(pl.multiple_of(((c * 2 + g) * half + y) * depth, depth), depth)
                edge = pl.ds(pl.multiple_of((c * half + y) * depth, depth), depth)
                for m in range(groups):
                    start = pl.multiple_of((me ^ m) * members, members)
                    near_left[pl.ds(start, members), near] = sources[m][c, 1 - g, first + y + 1]
                    left_ref[g, pl.ds(start, members), edge] = sources[m][c, g, first + y + 1]
                    at = (m * half + y) * members
                    put_images(
                        inner[at : at + members], label, density, near_right, start, near, count, materials
                    )

    part_ref[...] = correlate(near_left[...], near_right[...])


def vmem_spec():
    return pl.BlockSpec(memory_space=pltpu.VMEM)


def smem_spec():
    return pl.BlockSpec(memory_space=pltpu.SMEM)


def pack_kernel(pairs, me_ref, *refs):
    blocks = refs[:pairs]
    comps, planes, reach, members, depth = blocks[0].shape
    labelled = len(refs) > pairs + 2
    outs = refs[pairs + labelled : pairs + labelled + 2]
    half = (reach - 2) // 2
    for out, up in ((outs[0], 1 - me_ref[1]), (outs[1], me_ref[1])):
        first = (1 - up) * half
        for i, block in enumerate(blocks):
            for c in range(comps):
                out[i * comps + c] = block[c, up * (planes - 1), pl.ds(first, half + 2)]
        if labelled:
            labels_ref = refs[pairs]
            for y in range(half + 2):
                at = me_ref[0] * 2 * half + first + min(y, half - 1)
                row = labels_ref[up * (planes - 1), pl.ds(at, 1), :]
                out[pairs * comps, y] = jnp.broadcast_to(row, (members, depth)).astype(jnp.float32).astype(out.dtype)
    if labelled:
        put_stencil(refs[-1], planes)


def pack(pair, labels, me):
    comps, planes, reach, members, depth = pair[0].shape
    extra = [] if labels is None else [labels]
    out = jax.ShapeDtypeStruct(
        (len(pair) * comps + len(extra), (reach - 2) // 2 + 2, members, depth), pair[0].dtype
    )
    outs = [out, out]
    if extra:
        outs.append(jax.ShapeDtypeStruct((3 * planes * depth, 2 * planes * depth), pair[0].dtype))
    return pl.pallas_call(
        functools.partial(pack_kernel, len(pair)),
        out_shape=outs,
        in_specs=[smem_spec()] + [vmem_spec()] * (len(pair) + len(extra)),
        out_specs=[vmem_spec()] * len(outs),
        compiler_params=pltpu.CompilerParams(vmem_limit_bytes=16 * 2**20),
        cost_estimate=pl.CostEstimate(flops=0, bytes_accessed=2**20, transcendentals=0),
    )(me, *pair, *extra)


def local_tiles(blocks, labels, density, weights, me):
    groups = len(blocks)
    comps, planes, reach, members, depth = blocks[0].shape
    half = (reach - 2) // 2
    count = groups * members
    columns = (density.shape[0] + 1) * count
    image = jax.ShapeDtypeStruct((comps, 2, groups * half * members, 2 * depth), jnp.float32)
    return pl.pallas_call(
        functools.partial(local_kernel, groups, density.shape[0]),
        out_shape=[
            jax.ShapeDtypeStruct((count, columns), jnp.float32),
            image,
            image,
            jax.ShapeDtypeStruct((2, count, comps * half * depth), jnp.bfloat16),
        ],
        in_specs=[smem_spec(), smem_spec()] + [vmem_spec()] * (groups + 2),
        out_specs=[vmem_spec()] * 4,
        scratch_shapes=[
            pltpu.VMEM((count, comps * 2 * half * depth), jnp.bfloat16),
            pltpu.VMEM((columns, comps * 2 * half * depth), jnp.bfloat16),
        ],
        compiler_params=pltpu.CompilerParams(vmem_limit_bytes=40 * 2**20),
        cost_estimate=pl.CostEstimate(flops=5 * 10**9, bytes_accessed=12 * 2**20, transcendentals=0),
    )(me, density, *blocks, labels, weights)


def received_at(side, m, comps, c):
    part = 0
    while m >= side[part].shape[0] // comps:
        m -= side[part].shape[0] // comps
        part += 1
    return side[part].at[m * comps + c]


def returns_kernel(groups, materials, pairs, me_ref, density_ref, cross_ref, *refs):
    sides = (refs[:pairs], refs[pairs : 2 * pairs])
    below_ref, above_ref, left, right = refs[2 * pairs :]
    me = me_ref[0]
    comps = cross_ref.shape[0]
    reach, members, depth = sides[0][0].shape[1:]
    half = reach - 2
    count = groups * members

    @pl.loop(0, comps)
    def _(c):
        for side in range(2):
            g = me_ref[1] if side else 1 - me_ref[1]
            cross = cross_ref[c, g]
            for y in range(half):
                label = sides[side][0][sides[side][0].shape[0] - 1, y].astype(jnp.float32)
                density = density_at(label, density_ref, materials)
                lanes = pl.ds(pl.multiple_of((c * half + y) * depth, depth), depth)
                for m in range(groups):
                    start = pl.multiple_of((me ^ m) * members, members)
                    left[side, pl.ds(start, members), lanes] = received_at(sides[side], m, comps, c)[y + 1]
                    at = (m * half + y) * members
                    put_images(
                        cross[at : at + members], label, density, right.at[side], start, lanes, count, materials
                    )

    below_ref[...] = correlate(left[0], right[0])
    above_ref[...] = correlate(left[1], right[1])


def return_tiles(cross, lows, highs, density, me, groups):
    materials = density.shape[0]
    comps = cross.shape[0]
    reach, members, depth = lows[0].shape[1:]
    count = groups * members
    cells = comps * (reach - 2) * depth
    columns = (materials + 1) * count
    part = jax.ShapeDtypeStruct((count, columns), jnp.float32)
    halos = [*lows, *highs]
    return pl.pallas_call(
        functools.partial(returns_kernel, groups, materials, len(lows)),
        out_shape=[part, part],
        in_specs=[smem_spec(), smem_spec()] + [vmem_spec()] * (1 + len(halos)),
        out_specs=[vmem_spec()] * 2,
        scratch_shapes=[
            pltpu.VMEM((2, count, cells), jnp.bfloat16),
            pltpu.VMEM((2, columns, cells), jnp.bfloat16),
        ],
        compiler_params=pltpu.CompilerParams(vmem_limit_bytes=40 * 2**20),
        cost_estimate=pl.CostEstimate(flops=3 * 10**9, bytes_accessed=6 * 2**20, transcendentals=0),
    )(me, density, cross, *halos)


def edge_kernel(groups, materials, pairs, me_ref, density_ref, near_ref, edge_ref, left_ref, *refs):
    sides = (refs[:pairs], refs[pairs : 2 * pairs])
    labels_ref, weights_ref, part_ref, right = refs[2 * pairs :]
    me = me_ref[0]
    comps = edge_ref.shape[0]
    reach, members, depth = sides[0][0].shape[1:]
    half = reach - 2
    width = 2 * half
    count = groups * members

    @pl.loop(0, comps)
    def _(c):
        for side in range(2):
            g = me_ref[1] if side else 1 - me_ref[1]
            lhs = jnp.concatenate(
                [
                    jnp.concatenate(three_rows(received_at(sides[side], m, comps, c), 0, half), axis=1)
                    for m in range(groups)
                ],
                axis=0,
            )
            image = edge_ref[c, g] + jnp.dot(lhs, weights_ref[3 * depth : 6 * depth, : 2 * depth], preferred_element_type=jnp.float32)
            for y in range(half):
                label = labels_ref[g, pl.ds(me * width + g * half + y, 1), :]
                density = density_at(label, density_ref, materials)
                lanes = pl.ds(pl.multiple_of((c * half + y) * depth, depth), depth)
                for m in range(groups):
                    start = pl.multiple_of((me ^ m) * members, members)
                    at = (m * half + y) * members
                    put_images(
                        image[at : at + members], label, density, right.at[g], start, lanes, count, materials
                    )

    part_ref[...] = near_ref[...] + correlate(left_ref[0], right[0]) + correlate(left_ref[1], right[1])


def combine_kernel(part_ref, below_ref, above_ref, from_below_ref, from_above_ref, slab_ref, wide_ref):
    count = part_ref.shape[0]
    copies = wide_ref.shape[0] // count
    part = part_ref[...]
    slab_ref[...] = part + (from_below_ref[...] + from_above_ref[...])
    total = part + (below_ref[...] + above_ref[...])
    for s in range(count):
        for r in range(copies):
            wide_ref[s * copies + r] = total[s : s + 1]


def combine(part, returns, copies):
    count, columns = part.shape
    return pl.pallas_call(
        combine_kernel,
        out_shape=[
            jax.ShapeDtypeStruct((count, columns), jnp.float32),
            jax.ShapeDtypeStruct((count * copies, 1, columns), jnp.float32),
        ],
        in_specs=[vmem_spec()] * (1 + len(returns)),
        out_specs=[vmem_spec()] * 2,
        compiler_params=pltpu.CompilerParams(vmem_limit_bytes=16 * 2**20),
        cost_estimate=pl.CostEstimate(flops=0, bytes_accessed=2**19, transcendentals=0),
    )(part, *returns)


def edge_tiles(near, edge, left, lows, highs, labels, density, weights, me, groups):
    count, columns = near.shape
    materials = density.shape[0]
    part = jax.ShapeDtypeStruct((count, columns), jnp.float32)
    halos = [*lows, *highs]
    return pl.pallas_call(
        functools.partial(edge_kernel, groups, materials, len(lows)),
        out_shape=part,
        in_specs=[smem_spec(), smem_spec()] + [vmem_spec()] * (5 + len(halos)),
        out_specs=vmem_spec(),
        scratch_shapes=[pltpu.VMEM((2, columns, left.shape[2]), jnp.bfloat16)],
        compiler_params=pltpu.CompilerParams(vmem_limit_bytes=40 * 2**20),
        cost_estimate=pl.CostEstimate(flops=5 * 10**9, bytes_accessed=20 * 2**20, transcendentals=0),
    )(me, density, near, edge, left, *halos, labels, weights)


def finish_kernel(count, slab_scale, gram_scale, *refs):
    parts, rows_ref, slab_ref, gram_ref = refs[:-3], refs[-3], refs[-2], refs[-1]
    terms = [p[...] for p in parts]
    while len(terms) > 1:
        terms = [terms[i] + terms[i + 1] for i in range(0, len(terms), 2)]
    slab = terms[0] * slab_scale
    gram = jnp.sum(rows_ref[...], axis=0) * gram_scale
    for j in range(slab.shape[1] // count):
        slab_ref[0, j] = slab[:, j * count : (j + 1) * count]
        gram_ref[j] = gram[:, j * count : (j + 1) * count]


def finish(parts, rows, slab_scale, gram_scale):
    count, columns = parts[0].shape
    blocks = columns // count
    return pl.pallas_call(
        functools.partial(finish_kernel, count, slab_scale, gram_scale),
        out_shape=[
            jax.ShapeDtypeStruct((1, blocks, count, count), jnp.float32),
            jax.ShapeDtypeStruct((blocks, 1, count), jnp.float32),
        ],
        in_specs=[vmem_spec()] * (1 + len(parts)),
        out_specs=[vmem_spec()] * 2,
        compiler_params=pltpu.CompilerParams(vmem_limit_bytes=16 * 2**20),
    )(*parts, rows)


def body(snapshots, labels, free_mask, density):
    groups, slabs = lax.axis_size("snap"), lax.axis_size("space")
    planes, rows, depth = labels.shape
    me = jnp.stack([lax.axis_index("snap"), lax.axis_index("space") % 2]).astype(jnp.int32)
    with jax.named_scope("spread"):
        mine = spread(snapshots, free_mask, lax.axis_index("snap").astype(jnp.int32).reshape(1), groups)
    with jax.named_scope("regroup"):
        blocks = [mine[0]] + [
            lax.ppermute(mine[m], "snap", [(i, i ^ m) for i in range(groups)]) for m in range(1, groups)
        ]
    with jax.named_scope("halo"):
        even = [(i, i ^ 1) for i in range(slabs)]
        odd = [(i, ((i + 1) ^ 1) - 1) for i in range(1, slabs - 1)]
        firsts, seconds = [], []
        for start in range(0, groups, 2):
            some = blocks[start : start + 2]
            if firsts:
                some, *_ = lax.optimization_barrier((some, to_even, to_odd))
            to_even, to_odd, *stencil = pack(some, None if firsts else labels, me)
            if not firsts:
                weights = stencil[0]
                some, to_even, to_odd = lax.optimization_barrier((some, to_even, to_odd))
            seconds.append(lax.ppermute(to_odd, "space", odd))
            firsts.append(lax.ppermute(to_even, "space", even))
    with jax.named_scope("local_tiles"):
        near, edge, cross, left = local_tiles(blocks, labels, density, weights, me)
    with jax.named_scope("return_tiles"):
        below, above = return_tiles(cross, firsts, seconds, density, me, groups)
        from_below = lax.ppermute(below, "space", even)
        from_above = lax.ppermute(above, "space", odd)
    with jax.named_scope("edge_tiles"):
        part = edge_tiles(near, edge, left, firsts, seconds, labels, density, weights, me, groups)
    with jax.named_scope("sums"):
        part, wide = combine(part, (below, above, from_below, from_above), groups)
        sent = lax.all_to_all(wide, ("space", "snap"), 0, 0, tiled=True)
        parts = [part] + [
            lax.ppermute(part, "snap", [(i, i ^ m) for i in range(groups)]) for m in range(1, groups)
        ]
        slab_scale = 1.0 / (3.0 * planes * rows * depth)
        slab, gram = finish(parts, sent, slab_scale, slab_scale / slabs)
    return gram, slab


def solution(mesh):
    in_specs = (
        P("snap", None, "space", None, None),
        P("space", None, None),
        P("space", None, None),
        P(),
    )
    out_specs = (P(None, "space", None), P("space", None, None, None))
    return jax.shard_map(body, mesh=mesh, in_specs=in_specs, out_specs=out_specs, check_vma=False)
```

```python
import functools

import jax
import jax.numpy as jnp
import numpy as np
from jax import lax
from jax.experimental import pallas as pl
from jax.experimental.pallas import tpu as pltpu
from jax.sharding import PartitionSpec as P


def spread_kernel(groups, width, me_ref, snaps_ref, mask_ref, *refs):
    outs, turned = refs[:groups], refs[groups]
    rows = snaps_ref.shape[3]
    me = me_ref[0]
    mask = mask_ref[0].astype(jnp.float32)
    values = snaps_ref[:, 0, 0].astype(jnp.float32) * mask[None]
    edge = jnp.zeros(turned.shape[1:], turned.dtype)
    turned[0] = edge
    turned[rows + 1] = edge
    turned[1 : rows + 1] = jnp.swapaxes(values, 0, 1).astype(turned.dtype)
    for m in range(groups):
        outs[m][0, 0] = turned[pl.ds((me ^ m) * width, width + 2)]


def spread(snapshots, free_mask, me, groups):
    members, comps, planes, rows, depth = snapshots.shape
    width = rows // groups
    block = jax.ShapeDtypeStruct((comps, planes, width + 2, members, depth), snapshots.dtype)
    out_spec = pl.BlockSpec((1, 1, width + 2, members, depth), lambda c, p, me: (c, p, 0, 0, 0))
    return pl.pallas_call(
        functools.partial(spread_kernel, groups, width),
        out_shape=[block] * groups,
        grid_spec=pltpu.PrefetchScalarGridSpec(
            num_scalar_prefetch=1,
            grid=(comps, planes),
            in_specs=[
                pl.BlockSpec((members, 1, 1, rows, depth), lambda c, p, me: (0, c, p, 0, 0)),
                pl.BlockSpec((1, rows, depth), lambda c, p, me: (p, 0, 0)),
            ],
            out_specs=[out_spec] * groups,
            scratch_shapes=[pltpu.VMEM((rows + 2, members, depth), snapshots.dtype)],
        ),
        compiler_params=pltpu.CompilerParams(vmem_limit_bytes=32 * 2**20),
        cost_estimate=pl.CostEstimate(flops=0, bytes_accessed=5 * 2**20, transcendentals=0),
    )(me, snapshots, free_mask)


def put_stencil(weights_ref, planes):
    depth = weights_ref.shape[1] // (2 * planes)
    apart = jnp.abs(
        lax.broadcasted_iota(jnp.int32, (depth, depth), 0) - lax.broadcasted_iota(jnp.int32, (depth, depth), 1)
    )
    mass, stiff = (4.0, 1.0), (2.0, -1.0)
    for q in range(planes):
        for dy in range(3):
            for p in range(planes):
                x, y = abs(q - p), abs(dy - 1)
                both = mass[x] * mass[y]
                mixed = stiff[x] * mass[y] + mass[x] * stiff[y]
                for kind, (same, beside) in enumerate(
                    ((4.0 * both, both), (4.0 * mixed + 2.0 * both, mixed - both))
                ):
                    block = jnp.where(apart == 0, same, jnp.where(apart == 1, beside, 0.0))
                    weights_ref[
                        (q * 3 + dy) * depth : (q * 3 + dy + 1) * depth,
                        (p * 2 + kind) * depth : (p * 2 + kind + 1) * depth,
                    ] = block.astype(weights_ref.dtype)


def three_rows(block, first, height):
    members, depth = block.shape[-2:]
    return [block[first + dy : first + dy + height].reshape(height * members, depth) for dy in range(3)]


def at_cells(label, density_ref, materials, members):
    density = jnp.zeros(label.shape, jnp.float32)
    shown = []
    for j in range(materials):
        here = jnp.where(label == j, 1.0, 0.0)
        density = density + here * (density_ref[j] * (1.0 / 216.0))
        shown.append(jnp.broadcast_to(here, (members, label.shape[1])).astype(jnp.bfloat16))
    return density, shown


def put_images(image, shown, density, right, start, lanes, count):
    members, depth = image.shape[0], image.shape[1] // 2
    right[pl.ds(start, members), lanes] = (image[:, :depth] * density).astype(right.dtype)
    stiff = (image[:, depth:] * (1.0 / 36.0)).astype(right.dtype)
    for j, here in enumerate(shown):
        at = pl.multiple_of((j + 1) * count + start, members)
        right[pl.ds(at, members), lanes] = stiff * here


def correlate(left, right):
    return lax.dot_general(left, right, (((1,), (1,)), ((), ())), preferred_element_type=jnp.float32)


def local_kernel(groups, materials, me_ref, density_ref, *refs):
    sources = refs[:groups]
    labels_ref, weights_ref, part_ref, edge_ref, cross_ref, left_ref = refs[groups : groups + 6]
    scratch = refs[groups + 6 :]
    me = me_ref[0]
    comps, planes, reach, members, depth = sources[0].shape
    width = reach - 2
    half = width // 2
    count = groups * members
    wide = 2 * depth

    part = 0.0
    for c in range(comps):
        near_left, near_right = scratch[2 * c : 2 * c + 2]
        for g in range(2):
            first = g * half
            lhs = jnp.concatenate(
                [
                    jnp.concatenate(
                        [piece for p in range(planes) for piece in three_rows(source.at[c, p], first, half)], axis=1
                    )
                    for source in sources
                ],
                axis=0,
            )
            both = jnp.dot(lhs, weights_ref[...], preferred_element_type=jnp.float32)
            edge_ref[c, g] = both[:, g * wide : (g + 1) * wide]
            beside = weights_ref[3 * depth : 6 * depth, :wide]
            cross_ref[c, g] = jnp.dot(
                lhs[:, 3 * g * depth : 3 * (g + 1) * depth], beside, preferred_element_type=jnp.float32
            )
            inner = both[:, (1 - g) * wide : (2 - g) * wide]
            for y in range(half):
                label = labels_ref[1 - g, pl.ds(me * width + first + y, 1), :]
                density, shown = at_cells(label, density_ref, materials, members)
                near = slice((g * half + y) * depth, (g * half + y + 1) * depth)
                edge = slice((c * half + y) * depth, (c * half + y + 1) * depth)
                for m in range(groups):
                    start = pl.multiple_of((me ^ m) * members, members)
                    near_left[pl.ds(start, members), near] = sources[m][c, 1 - g, first + y + 1]
                    left_ref[g, pl.ds(start, members), edge] = sources[m][c, g, first + y + 1]
                    at = (m * half + y) * members
                    put_images(
                        inner[at : at + members], shown, density, near_right, start, near, count
                    )

        part = part + correlate(near_left[...], near_right[...])
    part_ref[...] = part


def vmem_spec():
    return pl.BlockSpec(memory_space=pltpu.VMEM)


def smem_spec():
    return pl.BlockSpec(memory_space=pltpu.SMEM)


def pack_kernel(pairs, me_ref, *refs):
    blocks = refs[:pairs]
    comps, planes, reach, members, depth = blocks[0].shape
    labelled = len(refs) > pairs + 2
    outs = refs[pairs + labelled : pairs + labelled + 2]
    half = (reach - 2) // 2
    for out, up in ((outs[0], 1 - me_ref[1]), (outs[1], me_ref[1])):
        first = (1 - up) * half
        for i, block in enumerate(blocks):
            for c in range(comps):
                out[i * comps + c] = block[c, up * (planes - 1), pl.ds(first, half + 2)]
        if labelled:
            labels_ref = refs[pairs]
            for y in range(half + 2):
                at = me_ref[0] * 2 * half + first + min(y, half - 1)
                row = labels_ref[up * (planes - 1), pl.ds(at, 1), :]
                out[pairs * comps, y] = jnp.broadcast_to(row, (members, depth)).astype(jnp.float32).astype(out.dtype)
    if labelled:
        put_stencil(refs[-1], planes)


def pack(pair, labels, me):
    comps, planes, reach, members, depth = pair[0].shape
    extra = [] if labels is None else [labels]
    out = jax.ShapeDtypeStruct(
        (len(pair) * comps + len(extra), (reach - 2) // 2 + 2, members, depth), pair[0].dtype
    )
    outs = [out, out]
    if extra:
        outs.append(jax.ShapeDtypeStruct((3 * planes * depth, 2 * planes * depth), pair[0].dtype))
    return pl.pallas_call(
        functools.partial(pack_kernel, len(pair)),
        out_shape=outs,
        in_specs=[smem_spec()] + [vmem_spec()] * (len(pair) + len(extra)),
        out_specs=[vmem_spec()] * len(outs),
        compiler_params=pltpu.CompilerParams(vmem_limit_bytes=16 * 2**20),
        cost_estimate=pl.CostEstimate(flops=0, bytes_accessed=2**20, transcendentals=0),
    )(me, *pair, *extra)


def local_tiles(blocks, labels, density, weights, me):
    groups = len(blocks)
    comps, planes, reach, members, depth = blocks[0].shape
    half = (reach - 2) // 2
    count = groups * members
    columns = (density.shape[0] + 1) * count
    image = jax.ShapeDtypeStruct((comps, 2, groups * half * members, 2 * depth), jnp.float32)
    return pl.pallas_call(
        functools.partial(local_kernel, groups, density.shape[0]),
        out_shape=[
            jax.ShapeDtypeStruct((count, columns), jnp.float32),
            image,
            image,
            jax.ShapeDtypeStruct((2, count, comps * half * depth), jnp.bfloat16),
        ],
        in_specs=[smem_spec(), smem_spec()] + [vmem_spec()] * (groups + 2),
        out_specs=[vmem_spec()] * 4,
        scratch_shapes=[
            pltpu.VMEM((count, 2 * half * depth), jnp.bfloat16),
            pltpu.VMEM((columns, 2 * half * depth), jnp.bfloat16),
        ]
        * comps,
        compiler_params=pltpu.CompilerParams(vmem_limit_bytes=40 * 2**20),
        cost_estimate=pl.CostEstimate(flops=5 * 10**9, bytes_accessed=12 * 2**20, transcendentals=0),
    )(me, density, *blocks, labels, weights)


def received_at(side, m, comps, c):
    part = 0
    while m >= side[part].shape[0] // comps:
        m -= side[part].shape[0] // comps
        part += 1
    return side[part].at[m * comps + c]


def returns_kernel(groups, materials, pairs, me_ref, density_ref, cross_ref, *refs):
    sides = (refs[:pairs], refs[pairs : 2 * pairs])
    below_ref, above_ref = refs[2 * pairs : 2 * pairs + 2]
    scratch = refs[2 * pairs + 2 :]
    me = me_ref[0]
    comps = cross_ref.shape[0]
    reach, members, depth = sides[0][0].shape[1:]
    half = reach - 2
    count = groups * members

    sums = [0.0, 0.0]
    for c in range(comps):
        for side in range(2):
            left, right = scratch[2 * (2 * c + side) : 2 * (2 * c + side) + 2]
            g = me_ref[1] if side else 1 - me_ref[1]
            cross = cross_ref[c, g]
            for y in range(half):
                label = sides[side][0][sides[side][0].shape[0] - 1, y].astype(jnp.float32)
                density, shown = at_cells(label, density_ref, materials, members)
                lanes = slice(y * depth, (y + 1) * depth)
                for m in range(groups):
                    start = pl.multiple_of((me ^ m) * members, members)
                    left[pl.ds(start, members), lanes] = received_at(sides[side], m, comps, c)[y + 1]
                    at = (m * half + y) * members
                    put_images(cross[at : at + members], shown, density, right, start, lanes, count)

            sums[side] = sums[side] + correlate(left[...], right[...])
    below_ref[...] = sums[0]
    above_ref[...] = sums[1]


def return_tiles(cross, lows, highs, density, me, groups):
    materials = density.shape[0]
    comps = cross.shape[0]
    reach, members, depth = lows[0].shape[1:]
    count = groups * members
    cells = comps * (reach - 2) * depth
    columns = (materials + 1) * count
    part = jax.ShapeDtypeStruct((count, columns), jnp.float32)
    halos = [*lows, *highs]
    return pl.pallas_call(
        functools.partial(returns_kernel, groups, materials, len(lows)),
        out_shape=[part, part],
        in_specs=[smem_spec(), smem_spec()] + [vmem_spec()] * (1 + len(halos)),
        out_specs=[vmem_spec()] * 2,
        scratch_shapes=[
            pltpu.VMEM((count, cells // comps), jnp.bfloat16),
            pltpu.VMEM((columns, cells // comps), jnp.bfloat16),
        ]
        * (2 * comps),
        compiler_params=pltpu.CompilerParams(vmem_limit_bytes=40 * 2**20),
        cost_estimate=pl.CostEstimate(flops=3 * 10**9, bytes_accessed=6 * 2**20, transcendentals=0),
    )(me, density, cross, *halos)


def edge_kernel(groups, materials, pairs, me_ref, density_ref, near_ref, edge_ref, left_ref, *refs):
    sides = (refs[:pairs], refs[pairs : 2 * pairs])
    labels_ref, weights_ref, part_ref = refs[2 * pairs : 2 * pairs + 3]
    rights = refs[2 * pairs + 3 :]
    me = me_ref[0]
    comps = edge_ref.shape[0]
    reach, members, depth = sides[0][0].shape[1:]
    half = reach - 2
    width = 2 * half
    count = groups * members

    part = near_ref[...]
    for c in range(comps):
        for side in range(2):
            right = rights[2 * c + side]
            g = me_ref[1] if side else 1 - me_ref[1]
            lhs = jnp.concatenate(
                [
                    jnp.concatenate(three_rows(received_at(sides[side], m, comps, c), 0, half), axis=1)
                    for m in range(groups)
                ],
                axis=0,
            )
            image = edge_ref[c, g] + jnp.dot(lhs, weights_ref[3 * depth : 6 * depth, : 2 * depth], preferred_element_type=jnp.float32)
            for y in range(half):
                label = labels_ref[g, pl.ds(me * width + g * half + y, 1), :]
                density, shown = at_cells(label, density_ref, materials, members)
                lanes = slice(y * depth, (y + 1) * depth)
                for m in range(groups):
                    start = pl.multiple_of((me ^ m) * members, members)
                    at = (m * half + y) * members
                    put_images(image[at : at + members], shown, density, right, start, lanes, count)

            part = part + correlate(left_ref[g, :, c * half * depth : (c + 1) * half * depth], right[...])
    part_ref[...] = part


def combine_kernel(part_ref, below_ref, above_ref, from_below_ref, from_above_ref, slab_ref, wide_ref):
    count = part_ref.shape[0]
    copies = wide_ref.shape[0] // count
    part = part_ref[...]
    slab_ref[...] = part + (from_below_ref[...] + from_above_ref[...])
    total = part + (below_ref[...] + above_ref[...])
    for s in range(count):
        for r in range(copies):
            wide_ref[s * copies + r] = total[s : s + 1]


def combine(part, returns, copies):
    count, columns = part.shape
    return pl.pallas_call(
        combine_kernel,
        out_shape=[
            jax.ShapeDtypeStruct((count, columns), jnp.float32),
            jax.ShapeDtypeStruct((count * copies, 1, columns), jnp.float32),
        ],
        in_specs=[vmem_spec()] * (1 + len(returns)),
        out_specs=[vmem_spec()] * 2,
        compiler_params=pltpu.CompilerParams(vmem_limit_bytes=16 * 2**20),
        cost_estimate=pl.CostEstimate(flops=0, bytes_accessed=2**19, transcendentals=0),
    )(part, *returns)


def edge_tiles(near, edge, left, lows, highs, labels, density, weights, me, groups):
    count, columns = near.shape
    materials = density.shape[0]
    part = jax.ShapeDtypeStruct((count, columns), jnp.float32)
    halos = [*lows, *highs]
    return pl.pallas_call(
        functools.partial(edge_kernel, groups, materials, len(lows)),
        out_shape=part,
        in_specs=[smem_spec(), smem_spec()] + [vmem_spec()] * (5 + len(halos)),
        out_specs=vmem_spec(),
        scratch_shapes=[pltpu.VMEM((columns, left.shape[2] // edge.shape[0]), jnp.bfloat16)] * (2 * edge.shape[0]),
        compiler_params=pltpu.CompilerParams(vmem_limit_bytes=40 * 2**20),
        cost_estimate=pl.CostEstimate(flops=5 * 10**9, bytes_accessed=20 * 2**20, transcendentals=0),
    )(me, density, near, edge, left, *halos, labels, weights)


def finish_kernel(count, slab_scale, gram_scale, *refs):
    parts, rows_ref, slab_ref, gram_ref = refs[:-3], refs[-3], refs[-2], refs[-1]
    terms = [p[...] for p in parts]
    while len(terms) > 1:
        terms = [terms[i] + terms[i + 1] for i in range(0, len(terms), 2)]
    slab = terms[0] * slab_scale
    gram = jnp.sum(rows_ref[...], axis=0) * gram_scale
    for j in range(slab.shape[1] // count):
        slab_ref[0, j] = slab[:, j * count : (j + 1) * count]
        gram_ref[j] = gram[:, j * count : (j + 1) * count]


def finish(parts, rows, slab_scale, gram_scale):
    count, columns = parts[0].shape
    blocks = columns // count
    return pl.pallas_call(
        functools.partial(finish_kernel, count, slab_scale, gram_scale),
        out_shape=[
            jax.ShapeDtypeStruct((1, blocks, count, count), jnp.float32),
            jax.ShapeDtypeStruct((blocks, 1, count), jnp.float32),
        ],
        in_specs=[vmem_spec()] * (1 + len(parts)),
        out_specs=[vmem_spec()] * 2,
        compiler_params=pltpu.CompilerParams(vmem_limit_bytes=16 * 2**20),
    )(*parts, rows)


def body(snapshots, labels, free_mask, density):
    groups, slabs = lax.axis_size("snap"), lax.axis_size("space")
    planes, rows, depth = labels.shape
    me = jnp.stack([lax.axis_index("snap"), lax.axis_index("space") % 2]).astype(jnp.int32)
    with jax.named_scope("spread"):
        mine = spread(snapshots, free_mask, lax.axis_index("snap").astype(jnp.int32).reshape(1), groups)
    with jax.named_scope("regroup"):
        blocks = [mine[0]] + [
            lax.ppermute(mine[m], "snap", [(i, i ^ m) for i in range(groups)]) for m in range(1, groups)
        ]
    with jax.named_scope("halo"):
        even = [(i, i ^ 1) for i in range(slabs)]
        odd = [(i, ((i + 1) ^ 1) - 1) for i in range(1, slabs - 1)]
        firsts, seconds = [], []
        for start in range(0, groups, 2):
            some = blocks[start : start + 2]
            if firsts:
                some, *_ = lax.optimization_barrier((some, to_even, to_odd))
            to_even, to_odd, *stencil = pack(some, None if firsts else labels, me)
            if not firsts:
                weights = stencil[0]
                some, to_even, to_odd = lax.optimization_barrier((some, to_even, to_odd))
            seconds.append(lax.ppermute(to_odd, "space", odd))
            firsts.append(lax.ppermute(to_even, "space", even))
    with jax.named_scope("local_tiles"):
        near, edge, cross, left = local_tiles(blocks, labels, density, weights, me)
    with jax.named_scope("return_tiles"):
        below, above = return_tiles(cross, firsts, seconds, density, me, groups)
        from_below = lax.ppermute(below, "space", even)
        from_above = lax.ppermute(above, "space", odd)
    with jax.named_scope("edge_tiles"):
        part = edge_tiles(near, edge, left, firsts, seconds, labels, density, weights, me, groups)
    with jax.named_scope("sums"):
        part, wide = combine(part, (below, above, from_below, from_above), groups)
        sent = lax.all_to_all(wide, ("space", "snap"), 0, 0, tiled=True)
        parts = [part] + [
            lax.ppermute(part, "snap", [(i, i ^ m) for i in range(groups)]) for m in range(1, groups)
        ]
        slab_scale = 1.0 / (3.0 * planes * rows * depth)
        slab, gram = finish(parts, sent, slab_scale, slab_scale / slabs)
    return gram, slab


def solution(mesh):
    in_specs = (
        P("snap", None, "space", None, None),
        P("space", None, None),
        P("space", None, None),
        P(),
    )
    out_specs = (P(None, "space", None), P("space", None, None, None))
    return jax.shard_map(body, mesh=mesh, in_specs=in_specs, out_specs=out_specs, check_vma=False)
```

```python
import functools

import jax
import jax.numpy as jnp
import numpy as np
from jax import lax
from jax.experimental import pallas as pl
from jax.experimental.pallas import tpu as pltpu
from jax.sharding import PartitionSpec as P


def spread_kernel(groups, width, me_ref, snaps_ref, mask_ref, *refs):
    outs, turned = refs[:groups], refs[groups]
    rows = snaps_ref.shape[3]
    me = me_ref[0]
    mask = mask_ref[0].astype(jnp.float32)
    values = snaps_ref[:, 0, 0].astype(jnp.float32) * mask[None]
    edge = jnp.zeros(turned.shape[1:], turned.dtype)
    turned[0] = edge
    turned[rows + 1] = edge
    turned[1 : rows + 1] = jnp.swapaxes(values, 0, 1).astype(turned.dtype)
    for m in range(groups):
        outs[m][0, 0] = turned[pl.ds((me ^ m) * width, width + 2)]


def spread(snapshots, free_mask, me, groups):
    members, comps, planes, rows, depth = snapshots.shape
    width = rows // groups
    block = jax.ShapeDtypeStruct((comps, planes, width + 2, members, depth), snapshots.dtype)
    out_spec = pl.BlockSpec((1, 1, width + 2, members, depth), lambda c, p, me: (c, p, 0, 0, 0))
    return pl.pallas_call(
        functools.partial(spread_kernel, groups, width),
        out_shape=[block] * groups,
        grid_spec=pltpu.PrefetchScalarGridSpec(
            num_scalar_prefetch=1,
            grid=(comps, planes),
            in_specs=[
                pl.BlockSpec((members, 1, 1, rows, depth), lambda c, p, me: (0, c, p, 0, 0)),
                pl.BlockSpec((1, rows, depth), lambda c, p, me: (p, 0, 0)),
            ],
            out_specs=[out_spec] * groups,
            scratch_shapes=[pltpu.VMEM((rows + 2, members, depth), snapshots.dtype)],
        ),
        compiler_params=pltpu.CompilerParams(vmem_limit_bytes=32 * 2**20),
        cost_estimate=pl.CostEstimate(flops=0, bytes_accessed=5 * 2**20, transcendentals=0),
    )(me, snapshots, free_mask)


def put_stencil(weights_ref, planes):
    depth = weights_ref.shape[1] // (2 * planes)
    apart = jnp.abs(
        lax.broadcasted_iota(jnp.int32, (depth, depth), 0) - lax.broadcasted_iota(jnp.int32, (depth, depth), 1)
    )
    mass, stiff = (4.0, 1.0), (2.0, -1.0)
    for q in range(planes):
        for dy in range(3):
            for p in range(planes):
                x, y = abs(q - p), abs(dy - 1)
                both = mass[x] * mass[y]
                mixed = stiff[x] * mass[y] + mass[x] * stiff[y]
                for kind, (same, beside) in enumerate(
                    ((4.0 * both, both), (4.0 * mixed + 2.0 * both, mixed - both))
                ):
                    block = jnp.where(apart == 0, same, jnp.where(apart == 1, beside, 0.0))
                    weights_ref[
                        (q * 3 + dy) * depth : (q * 3 + dy + 1) * depth,
                        (p * 2 + kind) * depth : (p * 2 + kind + 1) * depth,
                    ] = block.astype(weights_ref.dtype)


def three_rows(block, first, height):
    members, depth = block.shape[-2:]
    return [block[first + dy : first + dy + height].reshape(height * members, depth) for dy in range(3)]


def at_cells(label, density_ref, materials, members):
    density = jnp.zeros(label.shape, jnp.float32)
    shown = []
    for j in range(materials):
        here = jnp.where(label == j, 1.0, 0.0)
        density = density + here * (density_ref[j] * (1.0 / 216.0))
        shown.append(jnp.broadcast_to(here, (members, label.shape[1])).astype(jnp.bfloat16))
    return density, shown


def put_images(image, shown, density, right, start, lanes, count):
    members, depth = image.shape[0], image.shape[1] // 2
    right[pl.ds(start, members), lanes] = (image[:, :depth] * density).astype(right.dtype)
    stiff = (image[:, depth:] * (1.0 / 36.0)).astype(right.dtype)
    for j, here in enumerate(shown):
        at = pl.multiple_of((j + 1) * count + start, members)
        right[pl.ds(at, members), lanes] = stiff * here


def correlate(left, right):
    return lax.dot_general(left, right, (((1,), (1,)), ((), ())), preferred_element_type=jnp.float32)


def local_kernel(groups, materials, me_ref, density_ref, *refs):
    sources = refs[:groups]
    labels_ref, weights_ref, part_ref, edge_ref, cross_ref, left_ref = refs[groups : groups + 6]
    scratch = refs[groups + 6 :]
    me = me_ref[0]
    comps, planes, reach, members, depth = sources[0].shape
    width = reach - 2
    half = width // 2
    count = groups * members
    wide = 2 * depth

    part = 0.0
    for c in range(comps):
        near_left, near_right = scratch[2 * c : 2 * c + 2]
        for g in range(2):
            first = g * half
            lhs = jnp.concatenate(
                [
                    jnp.concatenate(
                        [piece for p in range(planes) for piece in three_rows(source.at[c, p], first, half)], axis=1
                    )
                    for source in sources
                ],
                axis=0,
            )
            both = jnp.dot(lhs, weights_ref[...], preferred_element_type=jnp.float32)
            edge_ref[c, g] = both[:, g * wide : (g + 1) * wide]
            beside = weights_ref[3 * depth : 6 * depth, :wide]
            cross_ref[c, g] = jnp.dot(
                lhs[:, 3 * g * depth : 3 * (g + 1) * depth], beside, preferred_element_type=jnp.float32
            )
            inner = both[:, (1 - g) * wide : (2 - g) * wide]
            for y in range(half):
                label = labels_ref[1 - g, pl.ds(me * width + first + y, 1), :]
                density, shown = at_cells(label, density_ref, materials, members)
                near = slice((g * half + y) * depth, (g * half + y + 1) * depth)
                edge = slice((c * half + y) * depth, (c * half + y + 1) * depth)
                for m in range(groups):
                    start = pl.multiple_of((me ^ m) * members, members)
                    near_left[pl.ds(start, members), near] = sources[m][c, 1 - g, first + y + 1]
                    left_ref[g, pl.ds(start, members), edge] = sources[m][c, g, first + y + 1]
                    at = (m * half + y) * members
                    put_images(
                        inner[at : at + members], shown, density, near_right, start, near, count
                    )

        part = part + correlate(near_left[...], near_right[...])
    part_ref[...] = part


def vmem_spec():
    return pl.BlockSpec(memory_space=pltpu.VMEM)


def smem_spec():
    return pl.BlockSpec(memory_space=pltpu.SMEM)


def pack_kernel(pairs, me_ref, *refs):
    blocks = refs[:pairs]
    comps, planes, reach, members, depth = blocks[0].shape
    labelled = len(refs) > pairs + 2
    outs = refs[pairs + labelled : pairs + labelled + 2]
    half = (reach - 2) // 2
    for out, up in ((outs[0], 1 - me_ref[1]), (outs[1], me_ref[1])):
        first = (1 - up) * half
        for i, block in enumerate(blocks):
            for c in range(comps):
                out[i * comps + c] = block[c, up * (planes - 1), pl.ds(first, half + 2)]
        if labelled:
            labels_ref = refs[pairs]
            for y in range(half + 2):
                at = me_ref[0] * 2 * half + first + min(y, half - 1)
                row = labels_ref[up * (planes - 1), pl.ds(at, 1), :]
                out[pairs * comps, y] = jnp.broadcast_to(row, (members, depth)).astype(jnp.float32).astype(out.dtype)
    if labelled:
        put_stencil(refs[-1], planes)


def pack(pair, labels, me):
    comps, planes, reach, members, depth = pair[0].shape
    extra = [] if labels is None else [labels]
    out = jax.ShapeDtypeStruct(
        (len(pair) * comps + len(extra), (reach - 2) // 2 + 2, members, depth), pair[0].dtype
    )
    outs = [out, out]
    if extra:
        outs.append(jax.ShapeDtypeStruct((3 * planes * depth, 2 * planes * depth), pair[0].dtype))
    return pl.pallas_call(
        functools.partial(pack_kernel, len(pair)),
        out_shape=outs,
        in_specs=[smem_spec()] + [vmem_spec()] * (len(pair) + len(extra)),
        out_specs=[vmem_spec()] * len(outs),
        compiler_params=pltpu.CompilerParams(vmem_limit_bytes=16 * 2**20),
        cost_estimate=pl.CostEstimate(flops=0, bytes_accessed=2**20, transcendentals=0),
    )(me, *pair, *extra)


def local_tiles(blocks, labels, density, weights, me):
    groups = len(blocks)
    comps, planes, reach, members, depth = blocks[0].shape
    half = (reach - 2) // 2
    count = groups * members
    columns = (density.shape[0] + 1) * count
    image = jax.ShapeDtypeStruct((comps, 2, groups * half * members, 2 * depth), jnp.float32)
    return pl.pallas_call(
        functools.partial(local_kernel, groups, density.shape[0]),
        out_shape=[
            jax.ShapeDtypeStruct((count, columns), jnp.float32),
            image,
            image,
            jax.ShapeDtypeStruct((2, count, comps * half * depth), jnp.bfloat16),
        ],
        in_specs=[smem_spec(), smem_spec()] + [vmem_spec()] * (groups + 2),
        out_specs=[vmem_spec()] * 4,
        scratch_shapes=[
            pltpu.VMEM((count, 2 * half * depth), jnp.bfloat16),
            pltpu.VMEM((columns, 2 * half * depth), jnp.bfloat16),
        ]
        * comps,
        compiler_params=pltpu.CompilerParams(vmem_limit_bytes=40 * 2**20),
        cost_estimate=pl.CostEstimate(flops=5 * 10**9, bytes_accessed=12 * 2**20, transcendentals=0),
    )(me, density, *blocks, labels, weights)


def received_at(side, m, comps, c):
    part = 0
    while m >= side[part].shape[0] // comps:
        m -= side[part].shape[0] // comps
        part += 1
    return side[part].at[m * comps + c]


def returns_kernel(groups, materials, pairs, me_ref, density_ref, cross_ref, *refs):
    sides = (refs[:pairs], refs[pairs : 2 * pairs])
    below_ref, above_ref = refs[2 * pairs : 2 * pairs + 2]
    scratch = refs[2 * pairs + 2 :]
    me = me_ref[0]
    comps = cross_ref.shape[0]
    reach, members, depth = sides[0][0].shape[1:]
    half = reach - 2
    count = groups * members

    sums = [0.0, 0.0]
    for c in range(comps):
        for side in range(2):
            left, right = scratch[2 * (2 * c + side) : 2 * (2 * c + side) + 2]
            g = me_ref[1] if side else 1 - me_ref[1]
            cross = cross_ref[c, g]
            for y in range(half):
                label = sides[side][0][sides[side][0].shape[0] - 1, y].astype(jnp.float32)
                density, shown = at_cells(label, density_ref, materials, members)
                lanes = slice(y * depth, (y + 1) * depth)
                for m in range(groups):
                    start = pl.multiple_of((me ^ m) * members, members)
                    left[pl.ds(start, members), lanes] = received_at(sides[side], m, comps, c)[y + 1]
                    at = (m * half + y) * members
                    put_images(cross[at : at + members], shown, density, right, start, lanes, count)

            sums[side] = sums[side] + correlate(left[...], right[...])
    below_ref[...] = sums[0]
    above_ref[...] = sums[1]


def return_tiles(cross, lows, highs, density, me, groups):
    materials = density.shape[0]
    comps = cross.shape[0]
    reach, members, depth = lows[0].shape[1:]
    count = groups * members
    cells = comps * (reach - 2) * depth
    columns = (materials + 1) * count
    part = jax.ShapeDtypeStruct((count, columns), jnp.float32)
    halos = [*lows, *highs]
    return pl.pallas_call(
        functools.partial(returns_kernel, groups, materials, len(lows)),
        out_shape=[part, part],
        in_specs=[smem_spec(), smem_spec()] + [vmem_spec()] * (1 + len(halos)),
        out_specs=[vmem_spec()] * 2,
        scratch_shapes=[
            pltpu.VMEM((count, cells // comps), jnp.bfloat16),
            pltpu.VMEM((columns, cells // comps), jnp.bfloat16),
        ]
        * (2 * comps),
        compiler_params=pltpu.CompilerParams(vmem_limit_bytes=40 * 2**20),
        cost_estimate=pl.CostEstimate(flops=3 * 10**9, bytes_accessed=6 * 2**20, transcendentals=0),
    )(me, density, cross, *halos)


def edge_kernel(groups, materials, pairs, me_ref, density_ref, near_ref, edge_ref, left_ref, *refs):
    sides = (refs[:pairs], refs[pairs : 2 * pairs])
    labels_ref, weights_ref, part_ref = refs[2 * pairs : 2 * pairs + 3]
    rights = refs[2 * pairs + 3 :]
    me = me_ref[0]
    comps = edge_ref.shape[0]
    reach, members, depth = sides[0][0].shape[1:]
    half = reach - 2
    width = 2 * half
    count = groups * members

    part = near_ref[...]
    for c in range(comps):
        for side in range(2):
            right = rights[2 * c + side]
            g = me_ref[1] if side else 1 - me_ref[1]
            lhs = jnp.concatenate(
                [
                    jnp.concatenate(three_rows(received_at(sides[side], m, comps, c), 0, half), axis=1)
                    for m in range(groups)
                ],
                axis=0,
            )
            image = edge_ref[c, g] + jnp.dot(lhs, weights_ref[3 * depth : 6 * depth, : 2 * depth], preferred_element_type=jnp.float32)
            for y in range(half):
                label = labels_ref[g, pl.ds(me * width + g * half + y, 1), :]
                density, shown = at_cells(label, density_ref, materials, members)
                lanes = slice(y * depth, (y + 1) * depth)
                for m in range(groups):
                    start = pl.multiple_of((me ^ m) * members, members)
                    at = (m * half + y) * members
                    put_images(image[at : at + members], shown, density, right, start, lanes, count)

            part = part + correlate(left_ref[g, :, c * half * depth : (c + 1) * half * depth], right[...])
    part_ref[...] = part


def combine_kernel(part_ref, below_ref, above_ref, from_below_ref, from_above_ref, slab_ref, wide_ref):
    count = part_ref.shape[0]
    copies = wide_ref.shape[0] // count
    part = part_ref[...]
    slab_ref[...] = part + (from_below_ref[...] + from_above_ref[...])
    total = part + (below_ref[...] + above_ref[...])
    depth = wide_ref.shape[2]
    for s in range(count):
        pieces = [total[s : s + 1, i * depth : (i + 1) * depth] for i in range(wide_ref.shape[1])]
        sent = jnp.concatenate(pieces, axis=0).astype(wide_ref.dtype)
        for r in range(copies):
            wide_ref[s * copies + r] = sent


def combine(part, returns, copies):
    count, columns = part.shape
    return pl.pallas_call(
        combine_kernel,
        out_shape=[
            jax.ShapeDtypeStruct((count, columns), jnp.float32),
            jax.ShapeDtypeStruct((count * copies, columns // 128, 128), jnp.bfloat16),
        ],
        in_specs=[vmem_spec()] * (1 + len(returns)),
        out_specs=[vmem_spec()] * 2,
        compiler_params=pltpu.CompilerParams(vmem_limit_bytes=16 * 2**20),
        cost_estimate=pl.CostEstimate(flops=0, bytes_accessed=2**19, transcendentals=0),
    )(part, *returns)


def edge_tiles(near, edge, left, lows, highs, labels, density, weights, me, groups):
    count, columns = near.shape
    materials = density.shape[0]
    part = jax.ShapeDtypeStruct((count, columns), jnp.float32)
    halos = [*lows, *highs]
    return pl.pallas_call(
        functools.partial(edge_kernel, groups, materials, len(lows)),
        out_shape=part,
        in_specs=[smem_spec(), smem_spec()] + [vmem_spec()] * (5 + len(halos)),
        out_specs=vmem_spec(),
        scratch_shapes=[pltpu.VMEM((columns, left.shape[2] // edge.shape[0]), jnp.bfloat16)] * (2 * edge.shape[0]),
        compiler_params=pltpu.CompilerParams(vmem_limit_bytes=40 * 2**20),
        cost_estimate=pl.CostEstimate(flops=5 * 10**9, bytes_accessed=20 * 2**20, transcendentals=0),
    )(me, density, near, edge, left, *halos, labels, weights)


def finish_kernel(count, slab_scale, gram_scale, *refs):
    parts, rows_ref, slab_ref, gram_ref = refs[:-3], refs[-3], refs[-2], refs[-1]
    terms = [p[...] for p in parts]
    while len(terms) > 1:
        terms = [terms[i] + terms[i + 1] for i in range(0, len(terms), 2)]
    slab = terms[0] * slab_scale
    gram = jnp.sum(rows_ref[...].astype(jnp.float32), axis=0) * gram_scale
    across = gram.shape[1] // count
    for j in range(slab.shape[1] // count):
        slab_ref[0, j] = slab[:, j * count : (j + 1) * count]
        gram_ref[j] = gram[j // across : j // across + 1, j % across * count : (j % across + 1) * count]


def finish(parts, rows, slab_scale, gram_scale):
    count, columns = parts[0].shape
    blocks = columns // count
    return pl.pallas_call(
        functools.partial(finish_kernel, count, slab_scale, gram_scale),
        out_shape=[
            jax.ShapeDtypeStruct((1, blocks, count, count), jnp.float32),
            jax.ShapeDtypeStruct((blocks, 1, count), jnp.float32),
        ],
        in_specs=[vmem_spec()] * (1 + len(parts)),
        out_specs=[vmem_spec()] * 2,
        compiler_params=pltpu.CompilerParams(vmem_limit_bytes=16 * 2**20),
    )(*parts, rows)


def body(snapshots, labels, free_mask, density):
    groups, slabs = lax.axis_size("snap"), lax.axis_size("space")
    planes, rows, depth = labels.shape
    me = jnp.stack([lax.axis_index("snap"), lax.axis_index("space") % 2]).astype(jnp.int32)
    with jax.named_scope("spread"):
        mine = spread(snapshots, free_mask, lax.axis_index("snap").astype(jnp.int32).reshape(1), groups)
    with jax.named_scope("regroup"):
        blocks = [mine[0]] + [
            lax.ppermute(mine[m], "snap", [(i, i ^ m) for i in range(groups)]) for m in range(1, groups)
        ]
    with jax.named_scope("halo"):
        even = [(i, i ^ 1) for i in range(slabs)]
        odd = [(i, ((i + 1) ^ 1) - 1) for i in range(1, slabs - 1)]
        firsts, seconds = [], []
        for start in range(0, groups, 2):
            some = blocks[start : start + 2]
            if firsts:
                some, *_ = lax.optimization_barrier((some, to_even, to_odd))
            to_even, to_odd, *stencil = pack(some, None if firsts else labels, me)
            if not firsts:
                weights = stencil[0]
                some, to_even, to_odd = lax.optimization_barrier((some, to_even, to_odd))
            seconds.append(lax.ppermute(to_odd, "space", odd))
            firsts.append(lax.ppermute(to_even, "space", even))
    with jax.named_scope("local_tiles"):
        near, edge, cross, left = local_tiles(blocks, labels, density, weights, me)
    with jax.named_scope("return_tiles"):
        below, above = return_tiles(cross, firsts, seconds, density, me, groups)
        from_below = lax.ppermute(below, "space", even)
        from_above = lax.ppermute(above, "space", odd)
    with jax.named_scope("edge_tiles"):
        part = edge_tiles(near, edge, left, firsts, seconds, labels, density, weights, me, groups)
    with jax.named_scope("sums"):
        part, wide = combine(part, (below, above, from_below, from_above), groups)
        sent = lax.all_to_all(wide, ("space", "snap"), 0, 0, tiled=True)
        parts = [part] + [
            lax.ppermute(part, "snap", [(i, i ^ m) for i in range(groups)]) for m in range(1, groups)
        ]
        slab_scale = 1.0 / (3.0 * planes * rows * depth)
        slab, gram = finish(parts, sent, slab_scale, slab_scale / slabs)
    return gram, slab


def solution(mesh):
    in_specs = (
        P("snap", None, "space", None, None),
        P("space", None, None),
        P("space", None, None),
        P(),
    )
    out_specs = (P(None, "space", None), P("space", None, None, None))
    return jax.shard_map(body, mesh=mesh, in_specs=in_specs, out_specs=out_specs, check_vma=False)
```

```python
import functools

import jax
import jax.numpy as jnp
import numpy as np
from jax import lax
from jax.experimental import pallas as pl
from jax.experimental.pallas import tpu as pltpu
from jax.sharding import PartitionSpec as P


def spread_kernel(groups, width, me_ref, snaps_ref, mask_ref, *refs):
    outs, turned = refs[:groups], refs[groups]
    rows = snaps_ref.shape[3]
    me = me_ref[0]
    mask = mask_ref[0].astype(jnp.float32)
    values = snaps_ref[:, 0, 0].astype(jnp.float32) * mask[None]
    edge = jnp.zeros(turned.shape[1:], turned.dtype)
    turned[0] = edge
    turned[rows + 1] = edge
    turned[1 : rows + 1] = jnp.swapaxes(values, 0, 1).astype(turned.dtype)
    for m in range(groups):
        outs[m][0, 0] = turned[pl.ds((me ^ m) * width, width + 2)]


def spread(snapshots, free_mask, me, groups):
    members, comps, planes, rows, depth = snapshots.shape
    width = rows // groups
    block = jax.ShapeDtypeStruct((comps, planes, width + 2, members, depth), snapshots.dtype)
    out_spec = pl.BlockSpec((1, 1, width + 2, members, depth), lambda c, p, me: (c, p, 0, 0, 0))
    return pl.pallas_call(
        functools.partial(spread_kernel, groups, width),
        out_shape=[block] * groups,
        grid_spec=pltpu.PrefetchScalarGridSpec(
            num_scalar_prefetch=1,
            grid=(comps, planes),
            in_specs=[
                pl.BlockSpec((members, 1, 1, rows, depth), lambda c, p, me: (0, c, p, 0, 0)),
                pl.BlockSpec((1, rows, depth), lambda c, p, me: (p, 0, 0)),
            ],
            out_specs=[out_spec] * groups,
            scratch_shapes=[pltpu.VMEM((rows + 2, members, depth), snapshots.dtype)],
        ),
        compiler_params=pltpu.CompilerParams(vmem_limit_bytes=32 * 2**20),
        cost_estimate=pl.CostEstimate(flops=0, bytes_accessed=5 * 2**20, transcendentals=0),
    )(me, snapshots, free_mask)


def put_stencil(weights_ref, planes):
    depth = weights_ref.shape[1] // (2 * planes)
    apart = jnp.abs(
        lax.broadcasted_iota(jnp.int32, (depth, depth), 0) - lax.broadcasted_iota(jnp.int32, (depth, depth), 1)
    )
    mass, stiff = (4.0, 1.0), (2.0, -1.0)
    for q in range(planes):
        for dy in range(3):
            for p in range(planes):
                x, y = abs(q - p), abs(dy - 1)
                both = mass[x] * mass[y]
                mixed = stiff[x] * mass[y] + mass[x] * stiff[y]
                for kind, (same, beside) in enumerate(
                    ((4.0 * both, both), (4.0 * mixed + 2.0 * both, mixed - both))
                ):
                    block = jnp.where(apart == 0, same, jnp.where(apart == 1, beside, 0.0))
                    weights_ref[
                        (q * 3 + dy) * depth : (q * 3 + dy + 1) * depth,
                        (p * 2 + kind) * depth : (p * 2 + kind + 1) * depth,
                    ] = block.astype(weights_ref.dtype)


def three_rows(block, first, height):
    members, depth = block.shape[-2:]
    return [block[first + dy : first + dy + height].reshape(height * members, depth) for dy in range(3)]


def at_cells(label, density_ref, materials, members):
    density = jnp.zeros(label.shape, jnp.float32)
    shown = []
    for j in range(materials):
        here = jnp.where(label == j, 1.0, 0.0)
        density = density + here * (density_ref[j] * (1.0 / 216.0))
        shown.append(jnp.broadcast_to(here, (members, label.shape[1])).astype(jnp.bfloat16))
    return density, shown


def put_images(image, shown, density, right, start, lanes, count):
    members, depth = image.shape[0], image.shape[1] // 2
    right[pl.ds(start, members), lanes] = (image[:, :depth] * density).astype(right.dtype)
    stiff = (image[:, depth:] * (1.0 / 36.0)).astype(right.dtype)
    for j, here in enumerate(shown):
        at = pl.multiple_of((j + 1) * count + start, members)
        right[pl.ds(at, members), lanes] = stiff * here


def correlate(left, right):
    return lax.dot_general(left, right, (((1,), (1,)), ((), ())), preferred_element_type=jnp.float32)


def local_kernel(groups, materials, me_ref, density_ref, *refs):
    sources = refs[:groups]
    labels_ref, weights_ref, part_ref, edge_ref, cross_ref, left_ref = refs[groups : groups + 6]
    scratch = refs[groups + 6 :]
    me = me_ref[0]
    comps, planes, reach, members, depth = sources[0].shape
    width = reach - 2
    half = width // 2
    count = groups * members
    wide = 2 * depth

    part = 0.0
    for c in range(comps):
        near_left, near_right = scratch[2 * c : 2 * c + 2]
        for g in range(2):
            first = g * half
            lhs = jnp.concatenate(
                [
                    jnp.concatenate(
                        [piece for p in range(planes) for piece in three_rows(source.at[c, p], first, half)], axis=1
                    )
                    for source in sources
                ],
                axis=0,
            )
            both = jnp.dot(lhs, weights_ref[...], preferred_element_type=jnp.float32)
            edge_ref[c, g] = both[:, g * wide : (g + 1) * wide]
            beside = weights_ref[3 * depth : 6 * depth, :wide]
            cross_ref[c, g] = jnp.dot(
                lhs[:, 3 * g * depth : 3 * (g + 1) * depth], beside, preferred_element_type=jnp.float32
            )
            inner = both[:, (1 - g) * wide : (2 - g) * wide]
            for y in range(half):
                label = labels_ref[1 - g, pl.ds(me * width + first + y, 1), :]
                density, shown = at_cells(label, density_ref, materials, members)
                near = slice((g * half + y) * depth, (g * half + y + 1) * depth)
                edge = slice((c * half + y) * depth, (c * half + y + 1) * depth)
                for m in range(groups):
                    start = pl.multiple_of((me ^ m) * members, members)
                    near_left[pl.ds(start, members), near] = sources[m][c, 1 - g, first + y + 1]
                    left_ref[g, pl.ds(start, members), edge] = sources[m][c, g, first + y + 1]
                    at = (m * half + y) * members
                    put_images(
                        inner[at : at + members], shown, density, near_right, start, near, count
                    )

        part = part + correlate(near_left[...], near_right[...])
    part_ref[...] = part


def vmem_spec():
    return pl.BlockSpec(memory_space=pltpu.VMEM)


def smem_spec():
    return pl.BlockSpec(memory_space=pltpu.SMEM)


def pack_kernel(pairs, me_ref, *refs):
    blocks = refs[:pairs]
    comps, planes, reach, members, depth = blocks[0].shape
    labelled = len(refs) > pairs + 2
    outs = refs[pairs + labelled : pairs + labelled + 2]
    half = (reach - 2) // 2
    for out, up in ((outs[0], 1 - me_ref[1]), (outs[1], me_ref[1])):
        first = (1 - up) * half
        for i, block in enumerate(blocks):
            for c in range(comps):
                out[i * comps + c] = block[c, up * (planes - 1), pl.ds(first, half + 2)]
        if labelled:
            labels_ref = refs[pairs]
            for y in range(half + 2):
                at = me_ref[0] * 2 * half + first + min(y, half - 1)
                row = labels_ref[up * (planes - 1), pl.ds(at, 1), :]
                out[pairs * comps, y] = jnp.broadcast_to(row, (members, depth)).astype(jnp.float32).astype(out.dtype)
    if labelled:
        put_stencil(refs[-1], planes)


def pack(pair, labels, me):
    comps, planes, reach, members, depth = pair[0].shape
    extra = [] if labels is None else [labels]
    out = jax.ShapeDtypeStruct(
        (len(pair) * comps + len(extra), (reach - 2) // 2 + 2, members, depth), pair[0].dtype
    )
    outs = [out, out]
    if extra:
        outs.append(jax.ShapeDtypeStruct((3 * planes * depth, 2 * planes * depth), pair[0].dtype))
    return pl.pallas_call(
        functools.partial(pack_kernel, len(pair)),
        out_shape=outs,
        in_specs=[smem_spec()] + [vmem_spec()] * (len(pair) + len(extra)),
        out_specs=[vmem_spec()] * len(outs),
        compiler_params=pltpu.CompilerParams(vmem_limit_bytes=16 * 2**20),
        cost_estimate=pl.CostEstimate(flops=0, bytes_accessed=2**20, transcendentals=0),
    )(me, *pair, *extra)


def local_tiles(blocks, labels, density, weights, me):
    groups = len(blocks)
    comps, planes, reach, members, depth = blocks[0].shape
    half = (reach - 2) // 2
    count = groups * members
    columns = (density.shape[0] + 1) * count
    image = jax.ShapeDtypeStruct((comps, 2, groups * half * members, 2 * depth), jnp.float32)
    return pl.pallas_call(
        functools.partial(local_kernel, groups, density.shape[0]),
        out_shape=[
            jax.ShapeDtypeStruct((count, columns), jnp.float32),
            image,
            image,
            jax.ShapeDtypeStruct((2, count, comps * half * depth), jnp.bfloat16),
        ],
        in_specs=[smem_spec(), smem_spec()] + [vmem_spec()] * (groups + 2),
        out_specs=[vmem_spec()] * 4,
        scratch_shapes=[
            pltpu.VMEM((count, 2 * half * depth), jnp.bfloat16),
            pltpu.VMEM((columns, 2 * half * depth), jnp.bfloat16),
        ]
        * comps,
        compiler_params=pltpu.CompilerParams(vmem_limit_bytes=40 * 2**20),
        cost_estimate=pl.CostEstimate(flops=5 * 10**9, bytes_accessed=12 * 2**20, transcendentals=0),
    )(me, density, *blocks, labels, weights)


def received_at(side, m, comps, c):
    part = 0
    while m >= side[part].shape[0] // comps:
        m -= side[part].shape[0] // comps
        part += 1
    return side[part].at[m * comps + c]


def returns_kernel(groups, materials, pairs, side, me_ref, density_ref, cross_ref, *refs):
    parts = refs[:pairs]
    back_ref, scratch = refs[pairs], refs[pairs + 1 :]
    me = me_ref[0]
    comps = cross_ref.shape[0]
    reach, members, depth = parts[0].shape[1:]
    half = reach - 2
    count = groups * members

    total = 0.0
    g = me_ref[1] if side else 1 - me_ref[1]
    for c in range(comps):
        left, right = scratch[2 * c : 2 * c + 2]
        cross = cross_ref[c, g]
        for y in range(half):
            label = parts[0][parts[0].shape[0] - 1, y].astype(jnp.float32)
            density, shown = at_cells(label, density_ref, materials, members)
            lanes = slice(y * depth, (y + 1) * depth)
            for m in range(groups):
                start = pl.multiple_of((me ^ m) * members, members)
                left[pl.ds(start, members), lanes] = received_at(parts, m, comps, c)[y + 1]
                at = (m * half + y) * members
                put_images(cross[at : at + members], shown, density, right, start, lanes, count)

        total = total + correlate(left[...], right[...])
    back_ref[...] = total


def return_tiles(cross, parts, side, density, me, groups):
    materials = density.shape[0]
    comps = cross.shape[0]
    reach, members, depth = parts[0].shape[1:]
    count = groups * members
    cells = comps * (reach - 2) * depth
    columns = (materials + 1) * count
    part = jax.ShapeDtypeStruct((count, columns), jnp.float32)
    return pl.pallas_call(
        functools.partial(returns_kernel, groups, materials, len(parts), side),
        out_shape=part,
        in_specs=[smem_spec(), smem_spec()] + [vmem_spec()] * (1 + len(parts)),
        out_specs=vmem_spec(),
        scratch_shapes=[
            pltpu.VMEM((count, cells // comps), jnp.bfloat16),
            pltpu.VMEM((columns, cells // comps), jnp.bfloat16),
        ]
        * comps,
        compiler_params=pltpu.CompilerParams(vmem_limit_bytes=40 * 2**20),
        cost_estimate=pl.CostEstimate(flops=3 * 10**9, bytes_accessed=6 * 2**20, transcendentals=0),
    )(me, density, cross, *parts)


def edge_kernel(groups, materials, pairs, me_ref, density_ref, near_ref, edge_ref, left_ref, *refs):
    sides = (refs[:pairs], refs[pairs : 2 * pairs])
    labels_ref, weights_ref, part_ref = refs[2 * pairs : 2 * pairs + 3]
    rights = refs[2 * pairs + 3 :]
    me = me_ref[0]
    comps = edge_ref.shape[0]
    reach, members, depth = sides[0][0].shape[1:]
    half = reach - 2
    width = 2 * half
    count = groups * members

    part = near_ref[...]
    for c in range(comps):
        for side in range(2):
            right = rights[2 * c + side]
            g = me_ref[1] if side else 1 - me_ref[1]
            lhs = jnp.concatenate(
                [
                    jnp.concatenate(three_rows(received_at(sides[side], m, comps, c), 0, half), axis=1)
                    for m in range(groups)
                ],
                axis=0,
            )
            image = edge_ref[c, g] + jnp.dot(lhs, weights_ref[3 * depth : 6 * depth, : 2 * depth], preferred_element_type=jnp.float32)
            for y in range(half):
                label = labels_ref[g, pl.ds(me * width + g * half + y, 1), :]
                density, shown = at_cells(label, density_ref, materials, members)
                lanes = slice(y * depth, (y + 1) * depth)
                for m in range(groups):
                    start = pl.multiple_of((me ^ m) * members, members)
                    at = (m * half + y) * members
                    put_images(image[at : at + members], shown, density, right, start, lanes, count)

            part = part + correlate(left_ref[g, :, c * half * depth : (c + 1) * half * depth], right[...])
    part_ref[...] = part


def combine_kernel(part_ref, below_ref, above_ref, from_below_ref, from_above_ref, slab_ref, wide_ref):
    count = part_ref.shape[0]
    copies = wide_ref.shape[0] // count
    part = part_ref[...]
    slab_ref[...] = part + (from_below_ref[...] + from_above_ref[...])
    total = part + (below_ref[...] + above_ref[...])
    depth = wide_ref.shape[2]
    for s in range(count):
        pieces = [total[s : s + 1, i * depth : (i + 1) * depth] for i in range(wide_ref.shape[1])]
        sent = jnp.concatenate(pieces, axis=0).astype(wide_ref.dtype)
        for r in range(copies):
            wide_ref[s * copies + r] = sent


def combine(part, returns, copies):
    count, columns = part.shape
    return pl.pallas_call(
        combine_kernel,
        out_shape=[
            jax.ShapeDtypeStruct((count, columns), jnp.float32),
            jax.ShapeDtypeStruct((count * copies, columns // 128, 128), jnp.bfloat16),
        ],
        in_specs=[vmem_spec()] * (1 + len(returns)),
        out_specs=[vmem_spec()] * 2,
        compiler_params=pltpu.CompilerParams(vmem_limit_bytes=16 * 2**20),
        cost_estimate=pl.CostEstimate(flops=0, bytes_accessed=2**19, transcendentals=0),
    )(part, *returns)


def edge_tiles(near, edge, left, lows, highs, labels, density, weights, me, groups):
    count, columns = near.shape
    materials = density.shape[0]
    part = jax.ShapeDtypeStruct((count, columns), jnp.float32)
    halos = [*lows, *highs]
    return pl.pallas_call(
        functools.partial(edge_kernel, groups, materials, len(lows)),
        out_shape=part,
        in_specs=[smem_spec(), smem_spec()] + [vmem_spec()] * (5 + len(halos)),
        out_specs=vmem_spec(),
        scratch_shapes=[pltpu.VMEM((columns, left.shape[2] // edge.shape[0]), jnp.bfloat16)] * (2 * edge.shape[0]),
        compiler_params=pltpu.CompilerParams(vmem_limit_bytes=40 * 2**20),
        cost_estimate=pl.CostEstimate(flops=5 * 10**9, bytes_accessed=20 * 2**20, transcendentals=0),
    )(me, density, near, edge, left, *halos, labels, weights)


def finish_kernel(count, slab_scale, gram_scale, *refs):
    parts, rows_ref, slab_ref, gram_ref = refs[:-3], refs[-3], refs[-2], refs[-1]
    terms = [p[...] for p in parts]
    while len(terms) > 1:
        terms = [terms[i] + terms[i + 1] for i in range(0, len(terms), 2)]
    slab = terms[0] * slab_scale
    gram = jnp.sum(rows_ref[...].astype(jnp.float32), axis=0) * gram_scale
    across = gram.shape[1] // count
    for j in range(slab.shape[1] // count):
        slab_ref[0, j] = slab[:, j * count : (j + 1) * count]
        gram_ref[j] = gram[j // across : j // across + 1, j % across * count : (j % across + 1) * count]


def finish(parts, rows, slab_scale, gram_scale):
    count, columns = parts[0].shape
    blocks = columns // count
    return pl.pallas_call(
        functools.partial(finish_kernel, count, slab_scale, gram_scale),
        out_shape=[
            jax.ShapeDtypeStruct((1, blocks, count, count), jnp.float32),
            jax.ShapeDtypeStruct((blocks, 1, count), jnp.float32),
        ],
        in_specs=[vmem_spec()] * (1 + len(parts)),
        out_specs=[vmem_spec()] * 2,
        compiler_params=pltpu.CompilerParams(vmem_limit_bytes=16 * 2**20),
    )(*parts, rows)


def body(snapshots, labels, free_mask, density):
    groups, slabs = lax.axis_size("snap"), lax.axis_size("space")
    planes, rows, depth = labels.shape
    me = jnp.stack([lax.axis_index("snap"), lax.axis_index("space") % 2]).astype(jnp.int32)
    with jax.named_scope("spread"):
        mine = spread(snapshots, free_mask, lax.axis_index("snap").astype(jnp.int32).reshape(1), groups)
    with jax.named_scope("regroup"):
        blocks = [mine[0]] + [
            lax.ppermute(mine[m], "snap", [(i, i ^ m) for i in range(groups)]) for m in range(1, groups)
        ]
    with jax.named_scope("halo"):
        even = [(i, i ^ 1) for i in range(slabs)]
        odd = [(i, ((i + 1) ^ 1) - 1) for i in range(1, slabs - 1)]
        firsts, seconds = [], []
        for start in range(0, groups, 2):
            some = blocks[start : start + 2]
            if firsts:
                some, *_ = lax.optimization_barrier((some, to_even, to_odd))
            to_even, to_odd, *stencil = pack(some, None if firsts else labels, me)
            if not firsts:
                weights = stencil[0]
                some, to_even, to_odd = lax.optimization_barrier((some, to_even, to_odd))
            seconds.append(lax.ppermute(to_odd, "space", odd))
            firsts.append(lax.ppermute(to_even, "space", even))
    with jax.named_scope("local_tiles"):
        near, edge, cross, left = local_tiles(blocks, labels, density, weights, me)
    with jax.named_scope("return_tiles"):
        above = return_tiles(cross, seconds, 1, density, me, groups)
        from_above = lax.ppermute(above, "space", odd)
        below = return_tiles(cross, firsts, 0, density, me, groups)
        from_below = lax.ppermute(below, "space", even)
    with jax.named_scope("edge_tiles"):
        part = edge_tiles(near, edge, left, firsts, seconds, labels, density, weights, me, groups)
    with jax.named_scope("sums"):
        part, wide = combine(part, (below, above, from_below, from_above), groups)
        sent = lax.all_to_all(wide, ("space", "snap"), 0, 0, tiled=True)
        parts = [part] + [
            lax.ppermute(part, "snap", [(i, i ^ m) for i in range(groups)]) for m in range(1, groups)
        ]
        slab_scale = 1.0 / (3.0 * planes * rows * depth)
        slab, gram = finish(parts, sent, slab_scale, slab_scale / slabs)
    return gram, slab


def solution(mesh):
    in_specs = (
        P("snap", None, "space", None, None),
        P("space", None, None),
        P("space", None, None),
        P(),
    )
    out_specs = (P(None, "space", None), P("space", None, None, None))
    return jax.shard_map(body, mesh=mesh, in_specs=in_specs, out_specs=out_specs, check_vma=False)
```

```python
import functools

import jax
import jax.numpy as jnp
import numpy as np
from jax import lax
from jax.experimental import pallas as pl
from jax.experimental.pallas import tpu as pltpu
from jax.sharding import PartitionSpec as P


def spread_kernel(groups, width, me_ref, snaps_ref, mask_ref, *refs):
    outs, turned = refs[:groups], refs[groups]
    rows = snaps_ref.shape[3]
    me = me_ref[0]
    mask = mask_ref[0].astype(jnp.float32)
    values = snaps_ref[:, 0, 0].astype(jnp.float32) * mask[None]
    edge = jnp.zeros(turned.shape[1:], turned.dtype)
    turned[0] = edge
    turned[rows + 1] = edge
    turned[1 : rows + 1] = jnp.swapaxes(values, 0, 1).astype(turned.dtype)
    for m in range(groups):
        outs[m][0, 0] = turned[pl.ds((me ^ m) * width, width + 2)]


def spread(snapshots, free_mask, me, groups):
    members, comps, planes, rows, depth = snapshots.shape
    width = rows // groups
    block = jax.ShapeDtypeStruct((comps, planes, width + 2, members, depth), snapshots.dtype)
    out_spec = pl.BlockSpec((1, 1, width + 2, members, depth), lambda c, p, me: (c, p, 0, 0, 0))
    return pl.pallas_call(
        functools.partial(spread_kernel, groups, width),
        out_shape=[block] * groups,
        grid_spec=pltpu.PrefetchScalarGridSpec(
            num_scalar_prefetch=1,
            grid=(comps, planes),
            in_specs=[
                pl.BlockSpec((members, 1, 1, rows, depth), lambda c, p, me: (0, c, p, 0, 0)),
                pl.BlockSpec((1, rows, depth), lambda c, p, me: (p, 0, 0)),
            ],
            out_specs=[out_spec] * groups,
            scratch_shapes=[pltpu.VMEM((rows + 2, members, depth), snapshots.dtype)],
        ),
        compiler_params=pltpu.CompilerParams(vmem_limit_bytes=32 * 2**20),
        cost_estimate=pl.CostEstimate(flops=0, bytes_accessed=5 * 2**20, transcendentals=0),
    )(me, snapshots, free_mask)


def put_stencil(weights_ref, planes):
    depth = weights_ref.shape[1] // (2 * planes)
    apart = jnp.abs(
        lax.broadcasted_iota(jnp.int32, (depth, depth), 0) - lax.broadcasted_iota(jnp.int32, (depth, depth), 1)
    )
    mass, stiff = (4.0, 1.0), (2.0, -1.0)
    for q in range(planes):
        for dy in range(3):
            for p in range(planes):
                x, y = abs(q - p), abs(dy - 1)
                both = mass[x] * mass[y]
                mixed = stiff[x] * mass[y] + mass[x] * stiff[y]
                for kind, (same, beside) in enumerate(
                    ((4.0 * both, both), (4.0 * mixed + 2.0 * both, mixed - both))
                ):
                    block = jnp.where(apart == 0, same, jnp.where(apart == 1, beside, 0.0))
                    weights_ref[
                        (q * 3 + dy) * depth : (q * 3 + dy + 1) * depth,
                        (p * 2 + kind) * depth : (p * 2 + kind + 1) * depth,
                    ] = block.astype(weights_ref.dtype)


def three_rows(block, first, height):
    members, depth = block.shape[-2:]
    return [block[first + dy : first + dy + height].reshape(height * members, depth) for dy in range(3)]


def at_cells(label, density_ref, materials, members):
    density = jnp.zeros(label.shape, jnp.float32)
    shown = []
    for j in range(materials):
        here = jnp.where(label == j, 1.0, 0.0)
        density = density + here * (density_ref[j] * (1.0 / 216.0))
        shown.append(jnp.broadcast_to(here, (members, label.shape[1])).astype(jnp.bfloat16))
    return density, shown


def put_images(image, shown, density, right, start, lanes, count):
    members, depth = image.shape[0], image.shape[1] // 2
    right[pl.ds(start, members), lanes] = (image[:, :depth] * density).astype(right.dtype)
    stiff = (image[:, depth:] * (1.0 / 36.0)).astype(right.dtype)
    for j, here in enumerate(shown):
        at = pl.multiple_of((j + 1) * count + start, members)
        right[pl.ds(at, members), lanes] = stiff * here


def correlate(left, right):
    return lax.dot_general(left, right, (((1,), (1,)), ((), ())), preferred_element_type=jnp.float32)


def local_kernel(groups, materials, me_ref, density_ref, *refs):
    sources = refs[:groups]
    labels_ref, weights_ref, part_ref, edge_ref, cross_ref, left_ref = refs[groups : groups + 6]
    scratch = refs[groups + 6 :]
    me = me_ref[0]
    comps, planes, reach, members, depth = sources[0].shape
    width = reach - 2
    half = width // 2
    count = groups * members
    wide = 2 * depth

    part = 0.0
    for c in range(comps):
        near_left, near_right = scratch[2 * c : 2 * c + 2]
        for g in range(2):
            first = g * half
            lhs = jnp.concatenate(
                [
                    jnp.concatenate(
                        [piece for p in range(planes) for piece in three_rows(source.at[c, p], first, half)], axis=1
                    )
                    for source in sources
                ],
                axis=0,
            )
            both = jnp.dot(lhs, weights_ref[...], preferred_element_type=jnp.float32)
            edge_ref[c, g] = both[:, g * wide : (g + 1) * wide]
            beside = weights_ref[3 * depth : 6 * depth, :wide]
            cross_ref[c, g] = jnp.dot(
                lhs[:, 3 * g * depth : 3 * (g + 1) * depth], beside, preferred_element_type=jnp.float32
            )
            inner = both[:, (1 - g) * wide : (2 - g) * wide]
            for y in range(half):
                label = labels_ref[1 - g, pl.ds(me * width + first + y, 1), :]
                density, shown = at_cells(label, density_ref, materials, members)
                near = slice((g * half + y) * depth, (g * half + y + 1) * depth)
                edge = slice((c * half + y) * depth, (c * half + y + 1) * depth)
                for m in range(groups):
                    start = pl.multiple_of((me ^ m) * members, members)
                    near_left[pl.ds(start, members), near] = sources[m][c, 1 - g, first + y + 1]
                    left_ref[g, pl.ds(start, members), edge] = sources[m][c, g, first + y + 1]
                    at = (m * half + y) * members
                    put_images(
                        inner[at : at + members], shown, density, near_right, start, near, count
                    )

        part = part + correlate(near_left[...], near_right[...])
    part_ref[...] = part


def vmem_spec():
    return pl.BlockSpec(memory_space=pltpu.VMEM)


def smem_spec():
    return pl.BlockSpec(memory_space=pltpu.SMEM)


def pack_kernel(pairs, me_ref, *refs):
    blocks = refs[:pairs]
    comps, planes, reach, members, depth = blocks[0].shape
    labelled = len(refs) > pairs + 2
    outs = refs[pairs + labelled : pairs + labelled + 2]
    half = (reach - 2) // 2
    for out, up in ((outs[0], 1 - me_ref[1]), (outs[1], me_ref[1])):
        first = (1 - up) * half
        for i, block in enumerate(blocks):
            for c in range(comps):
                out[i * comps + c] = block[c, up * (planes - 1), pl.ds(first, half + 2)]
        if labelled:
            labels_ref = refs[pairs]
            for y in range(half + 2):
                at = me_ref[0] * 2 * half + first + min(y, half - 1)
                row = labels_ref[up * (planes - 1), pl.ds(at, 1), :]
                out[pairs * comps, y] = jnp.broadcast_to(row, (members, depth)).astype(jnp.float32).astype(out.dtype)
    if labelled:
        put_stencil(refs[-1], planes)


def pack(pair, labels, me):
    comps, planes, reach, members, depth = pair[0].shape
    extra = [] if labels is None else [labels]
    out = jax.ShapeDtypeStruct(
        (len(pair) * comps + len(extra), (reach - 2) // 2 + 2, members, depth), pair[0].dtype
    )
    outs = [out, out]
    if extra:
        outs.append(jax.ShapeDtypeStruct((3 * planes * depth, 2 * planes * depth), pair[0].dtype))
    return pl.pallas_call(
        functools.partial(pack_kernel, len(pair)),
        out_shape=outs,
        in_specs=[smem_spec()] + [vmem_spec()] * (len(pair) + len(extra)),
        out_specs=[vmem_spec()] * len(outs),
        compiler_params=pltpu.CompilerParams(vmem_limit_bytes=16 * 2**20),
        cost_estimate=pl.CostEstimate(flops=0, bytes_accessed=2**20, transcendentals=0),
    )(me, *pair, *extra)


def local_tiles(blocks, labels, density, weights, me):
    groups = len(blocks)
    comps, planes, reach, members, depth = blocks[0].shape
    half = (reach - 2) // 2
    count = groups * members
    columns = (density.shape[0] + 1) * count
    image = jax.ShapeDtypeStruct((comps, 2, groups * half * members, 2 * depth), jnp.float32)
    return pl.pallas_call(
        functools.partial(local_kernel, groups, density.shape[0]),
        out_shape=[
            jax.ShapeDtypeStruct((count, columns), jnp.float32),
            image,
            image,
            jax.ShapeDtypeStruct((2, count, comps * half * depth), jnp.bfloat16),
        ],
        in_specs=[smem_spec(), smem_spec()] + [vmem_spec()] * (groups + 2),
        out_specs=[vmem_spec()] * 4,
        scratch_shapes=[
            pltpu.VMEM((count, 2 * half * depth), jnp.bfloat16),
            pltpu.VMEM((columns, 2 * half * depth), jnp.bfloat16),
        ]
        * comps,
        compiler_params=pltpu.CompilerParams(vmem_limit_bytes=40 * 2**20),
        cost_estimate=pl.CostEstimate(flops=5 * 10**9, bytes_accessed=12 * 2**20, transcendentals=0),
    )(me, density, *blocks, labels, weights)


def received_at(side, m, comps, c):
    part = 0
    while m >= side[part].shape[0] // comps:
        m -= side[part].shape[0] // comps
        part += 1
    return side[part].at[m * comps + c]


def returns_kernel(groups, materials, pairs, side, me_ref, density_ref, cross_ref, *refs):
    parts = refs[:pairs]
    back_ref, scratch = refs[pairs], refs[pairs + 1 :]
    me = me_ref[0]
    comps = cross_ref.shape[0]
    reach, members, depth = parts[0].shape[1:]
    half = reach - 2
    count = groups * members

    total = 0.0
    g = me_ref[1] if side else 1 - me_ref[1]
    for c in range(comps):
        left, right = scratch[2 * c : 2 * c + 2]
        cross = cross_ref[c, g]
        for y in range(half):
            label = parts[0][parts[0].shape[0] - 1, y].astype(jnp.float32)
            density, shown = at_cells(label, density_ref, materials, members)
            lanes = slice(y * depth, (y + 1) * depth)
            for m in range(groups):
                start = pl.multiple_of((me ^ m) * members, members)
                left[pl.ds(start, members), lanes] = received_at(parts, m, comps, c)[y + 1]
                at = (m * half + y) * members
                put_images(cross[at : at + members], shown, density, right, start, lanes, count)

        total = total + correlate(left[...], right[...])
    back_ref[...] = total


def return_tiles(cross, parts, side, density, me, groups):
    materials = density.shape[0]
    comps = cross.shape[0]
    reach, members, depth = parts[0].shape[1:]
    count = groups * members
    cells = comps * (reach - 2) * depth
    columns = (materials + 1) * count
    part = jax.ShapeDtypeStruct((count, columns), jnp.float32)
    return pl.pallas_call(
        functools.partial(returns_kernel, groups, materials, len(parts), side),
        out_shape=part,
        in_specs=[smem_spec(), smem_spec()] + [vmem_spec()] * (1 + len(parts)),
        out_specs=vmem_spec(),
        scratch_shapes=[
            pltpu.VMEM((count, cells // comps), jnp.bfloat16),
            pltpu.VMEM((columns, cells // comps), jnp.bfloat16),
        ]
        * comps,
        compiler_params=pltpu.CompilerParams(vmem_limit_bytes=40 * 2**20),
        cost_estimate=pl.CostEstimate(flops=3 * 10**9, bytes_accessed=6 * 2**20, transcendentals=0),
    )(me, density, cross, *parts)


def edge_kernel(groups, materials, pairs, me_ref, density_ref, near_ref, edge_ref, left_ref, *refs):
    sides = (refs[:pairs], refs[pairs : 2 * pairs])
    labels_ref, weights_ref, part_ref = refs[2 * pairs : 2 * pairs + 3]
    rights = refs[2 * pairs + 3 :]
    me = me_ref[0]
    comps = edge_ref.shape[0]
    reach, members, depth = sides[0][0].shape[1:]
    half = reach - 2
    width = 2 * half
    count = groups * members

    part = near_ref[...]
    for c in range(comps):
        for side in range(2):
            right = rights[2 * c + side]
            g = me_ref[1] if side else 1 - me_ref[1]
            lhs = jnp.concatenate(
                [
                    jnp.concatenate(three_rows(received_at(sides[side], m, comps, c), 0, half), axis=1)
                    for m in range(groups)
                ],
                axis=0,
            )
            image = edge_ref[c, g] + jnp.dot(lhs, weights_ref[3 * depth : 6 * depth, : 2 * depth], preferred_element_type=jnp.float32)
            for y in range(half):
                label = labels_ref[g, pl.ds(me * width + g * half + y, 1), :]
                density, shown = at_cells(label, density_ref, materials, members)
                lanes = slice(y * depth, (y + 1) * depth)
                for m in range(groups):
                    start = pl.multiple_of((me ^ m) * members, members)
                    at = (m * half + y) * members
                    put_images(image[at : at + members], shown, density, right, start, lanes, count)

            part = part + correlate(left_ref[g, :, c * half * depth : (c + 1) * half * depth], right[...])
    part_ref[...] = part


def combine_kernel(part_ref, below_ref, above_ref, from_below_ref, from_above_ref, slab_ref, wide_ref):
    count = part_ref.shape[0]
    copies = wide_ref.shape[0] // count
    part = part_ref[...]
    slab_ref[...] = part + (from_below_ref[...] + from_above_ref[...])
    total = part + (below_ref[...] + above_ref[...])
    depth = wide_ref.shape[2]
    for s in range(count):
        pieces = [total[s : s + 1, i * depth : (i + 1) * depth] for i in range(wide_ref.shape[1])]
        sent = jnp.concatenate(pieces, axis=0).astype(wide_ref.dtype)
        for r in range(copies):
            wide_ref[s * copies + r] = sent


def combine(part, returns, copies):
    count, columns = part.shape
    return pl.pallas_call(
        combine_kernel,
        out_shape=[
            jax.ShapeDtypeStruct((count, columns), jnp.float32),
            jax.ShapeDtypeStruct((count * copies, columns // 128, 128), jnp.bfloat16),
        ],
        in_specs=[vmem_spec()] * (1 + len(returns)),
        out_specs=[vmem_spec()] * 2,
        compiler_params=pltpu.CompilerParams(vmem_limit_bytes=16 * 2**20),
        cost_estimate=pl.CostEstimate(flops=0, bytes_accessed=2**19, transcendentals=0),
    )(part, *returns)


def edge_tiles(near, edge, left, lows, highs, labels, density, weights, me, groups):
    count, columns = near.shape
    materials = density.shape[0]
    part = jax.ShapeDtypeStruct((count, columns), jnp.float32)
    halos = [*lows, *highs]
    return pl.pallas_call(
        functools.partial(edge_kernel, groups, materials, len(lows)),
        out_shape=part,
        in_specs=[smem_spec(), smem_spec()] + [vmem_spec()] * (5 + len(halos)),
        out_specs=vmem_spec(),
        scratch_shapes=[pltpu.VMEM((columns, left.shape[2] // edge.shape[0]), jnp.bfloat16)] * (2 * edge.shape[0]),
        compiler_params=pltpu.CompilerParams(vmem_limit_bytes=40 * 2**20),
        cost_estimate=pl.CostEstimate(flops=5 * 10**9, bytes_accessed=20 * 2**20, transcendentals=0),
    )(me, density, near, edge, left, *halos, labels, weights)


def finish_kernel(count, slab_scale, gram_scale, *refs):
    parts, rows_ref, slab_ref, gram_ref = refs[:-3], refs[-3], refs[-2], refs[-1]
    terms = [p[...] for p in parts]
    while len(terms) > 1:
        terms = [terms[i] + terms[i + 1] for i in range(0, len(terms), 2)]
    slab = terms[0] * slab_scale
    gram = jnp.sum(rows_ref[...].astype(jnp.float32), axis=0) * gram_scale
    across = gram.shape[1] // count
    for j in range(slab.shape[1] // count):
        slab_ref[0, j] = slab[:, j * count : (j + 1) * count]
        gram_ref[j] = gram[j // across : j // across + 1, j % across * count : (j % across + 1) * count]


def finish(parts, rows, slab_scale, gram_scale):
    count, columns = parts[0].shape
    blocks = columns // count
    return pl.pallas_call(
        functools.partial(finish_kernel, count, slab_scale, gram_scale),
        out_shape=[
            jax.ShapeDtypeStruct((1, blocks, count, count), jnp.float32),
            jax.ShapeDtypeStruct((blocks, 1, count), jnp.float32),
        ],
        in_specs=[vmem_spec()] * (1 + len(parts)),
        out_specs=[vmem_spec()] * 2,
        compiler_params=pltpu.CompilerParams(vmem_limit_bytes=16 * 2**20),
    )(*parts, rows)


def body(snapshots, labels, free_mask, density):
    groups, slabs = lax.axis_size("snap"), lax.axis_size("space")
    planes, rows, depth = labels.shape
    me = jnp.stack([lax.axis_index("snap"), lax.axis_index("space") % 2]).astype(jnp.int32)
    with jax.named_scope("spread"):
        mine = spread(snapshots, free_mask, lax.axis_index("snap").astype(jnp.int32).reshape(1), groups)
    with jax.named_scope("regroup"):
        blocks = [mine[0]] + [
            lax.ppermute(mine[m], "snap", [(i, i ^ m) for i in range(groups)]) for m in range(1, groups)
        ]
    with jax.named_scope("halo"):
        even = [(i, i ^ 1) for i in range(slabs)]
        odd = [(i, ((i + 1) ^ 1) - 1) for i in range(1, slabs - 1)]
        firsts, seconds = [], []
        for start in range(0, groups, 2):
            some = blocks[start : start + 2]
            if firsts:
                some, *_ = lax.optimization_barrier((some, to_even, to_odd))
            to_even, to_odd, *stencil = pack(some, None if firsts else labels, me)
            if not firsts:
                weights = stencil[0]
                some, to_even, to_odd = lax.optimization_barrier((some, to_even, to_odd))
            seconds.append(lax.ppermute(to_odd, "space", odd))
            firsts.append(lax.ppermute(to_even, "space", even))
    with jax.named_scope("local_tiles"):
        near, edge, cross, left = local_tiles(blocks, labels, density, weights, me)
    with jax.named_scope("return_tiles"):
        above = return_tiles(cross, seconds, 1, density, me, groups)
        from_above = lax.ppermute(above, "space", odd)
        firsts, above = lax.optimization_barrier((firsts, above))
        below = return_tiles(cross, firsts, 0, density, me, groups)
        from_below = lax.ppermute(below, "space", even)
    with jax.named_scope("edge_tiles"):
        part = edge_tiles(near, edge, left, firsts, seconds, labels, density, weights, me, groups)
    with jax.named_scope("sums"):
        part, wide = combine(part, (below, above, from_below, from_above), groups)
        sent = lax.all_to_all(wide, ("space", "snap"), 0, 0, tiled=True)
        parts = [part] + [
            lax.ppermute(part, "snap", [(i, i ^ m) for i in range(groups)]) for m in range(1, groups)
        ]
        slab_scale = 1.0 / (3.0 * planes * rows * depth)
        slab, gram = finish(parts, sent, slab_scale, slab_scale / slabs)
    return gram, slab


def solution(mesh):
    in_specs = (
        P("snap", None, "space", None, None),
        P("space", None, None),
        P("space", None, None),
        P(),
    )
    out_specs = (P(None, "space", None), P("space", None, None, None))
    return jax.shard_map(body, mesh=mesh, in_specs=in_specs, out_specs=out_specs, check_vma=False)
```

```python
import functools

import jax
import jax.numpy as jnp
import numpy as np
from jax import lax
from jax.experimental import pallas as pl
from jax.experimental.pallas import tpu as pltpu
from jax.sharding import PartitionSpec as P


def spread_kernel(groups, width, me_ref, snaps_ref, mask_ref, *refs):
    outs, turned = refs[:groups], refs[groups]
    rows = snaps_ref.shape[3]
    me = me_ref[0]
    mask = mask_ref[0].astype(jnp.float32)
    values = snaps_ref[:, 0, 0].astype(jnp.float32) * mask[None]
    edge = jnp.zeros(turned.shape[1:], turned.dtype)
    turned[0] = edge
    turned[rows + 1] = edge
    turned[1 : rows + 1] = jnp.swapaxes(values, 0, 1).astype(turned.dtype)
    for m in range(groups):
        outs[m][0, 0] = turned[pl.ds((me ^ m) * width, width + 2)]


def spread(snapshots, free_mask, me, groups):
    members, comps, planes, rows, depth = snapshots.shape
    width = rows // groups
    block = jax.ShapeDtypeStruct((comps, planes, width + 2, members, depth), snapshots.dtype)
    out_spec = pl.BlockSpec((1, 1, width + 2, members, depth), lambda c, p, me: (c, p, 0, 0, 0))
    return pl.pallas_call(
        functools.partial(spread_kernel, groups, width),
        out_shape=[block] * groups,
        grid_spec=pltpu.PrefetchScalarGridSpec(
            num_scalar_prefetch=1,
            grid=(comps, planes),
            in_specs=[
                pl.BlockSpec((members, 1, 1, rows, depth), lambda c, p, me: (0, c, p, 0, 0)),
                pl.BlockSpec((1, rows, depth), lambda c, p, me: (p, 0, 0)),
            ],
            out_specs=[out_spec] * groups,
            scratch_shapes=[pltpu.VMEM((rows + 2, members, depth), snapshots.dtype)],
        ),
        compiler_params=pltpu.CompilerParams(vmem_limit_bytes=32 * 2**20),
        cost_estimate=pl.CostEstimate(flops=0, bytes_accessed=5 * 2**20, transcendentals=0),
    )(me, snapshots, free_mask)


def put_stencil(weights_ref, planes):
    depth = weights_ref.shape[1] // (2 * planes)
    apart = jnp.abs(
        lax.broadcasted_iota(jnp.int32, (depth, depth), 0) - lax.broadcasted_iota(jnp.int32, (depth, depth), 1)
    )
    mass, stiff = (4.0, 1.0), (2.0, -1.0)
    for q in range(planes):
        for dy in range(3):
            for p in range(planes):
                x, y = abs(q - p), abs(dy - 1)
                both = mass[x] * mass[y]
                mixed = stiff[x] * mass[y] + mass[x] * stiff[y]
                for kind, (same, beside) in enumerate(
                    ((4.0 * both, both), (4.0 * mixed + 2.0 * both, mixed - both))
                ):
                    block = jnp.where(apart == 0, same, jnp.where(apart == 1, beside, 0.0))
                    weights_ref[
                        (q * 3 + dy) * depth : (q * 3 + dy + 1) * depth,
                        (p * 2 + kind) * depth : (p * 2 + kind + 1) * depth,
                    ] = block.astype(weights_ref.dtype)


def three_rows(block, first, height):
    members, depth = block.shape[-2:]
    return [block[first + dy : first + dy + height].reshape(height * members, depth) for dy in range(3)]


def at_cells(label, density_ref, materials, members):
    density = jnp.zeros(label.shape, jnp.float32)
    shown = []
    for j in range(materials):
        here = jnp.where(label == j, 1.0, 0.0)
        density = density + here * (density_ref[j] * (1.0 / 216.0))
        shown.append(jnp.broadcast_to(here, (members, label.shape[1])).astype(jnp.bfloat16))
    return density, shown


def put_images(image, shown, density, right, start, lanes, count):
    members, depth = image.shape[0], image.shape[1] // 2
    right[pl.ds(start, members), lanes] = (image[:, :depth] * density).astype(right.dtype)
    stiff = (image[:, depth:] * (1.0 / 36.0)).astype(right.dtype)
    for j, here in enumerate(shown):
        at = pl.multiple_of((j + 1) * count + start, members)
        right[pl.ds(at, members), lanes] = stiff * here


def correlate(left, right):
    return lax.dot_general(left, right, (((1,), (1,)), ((), ())), preferred_element_type=jnp.float32)


def local_kernel(groups, materials, me_ref, density_ref, *refs):
    sources = refs[:groups]
    labels_ref, weights_ref, part_ref, edge_ref, cross_ref, left_ref = refs[groups : groups + 6]
    scratch = refs[groups + 6 :]
    me = me_ref[0]
    comps, planes, reach, members, depth = sources[0].shape
    width = reach - 2
    half = width // 2
    count = groups * members
    wide = 2 * depth

    part = 0.0
    for c in range(comps):
        near_left, near_right = scratch[2 * c : 2 * c + 2]
        for g in range(2):
            first = g * half
            lhs = jnp.concatenate(
                [
                    jnp.concatenate(
                        [piece for p in range(planes) for piece in three_rows(source.at[c, p], first, half)], axis=1
                    )
                    for source in sources
                ],
                axis=0,
            )
            both = jnp.dot(lhs, weights_ref[...], preferred_element_type=jnp.float32)
            edge_ref[c, g] = both[:, g * wide : (g + 1) * wide]
            beside = weights_ref[3 * depth : 6 * depth, :wide]
            cross_ref[c, g] = jnp.dot(
                lhs[:, 3 * g * depth : 3 * (g + 1) * depth], beside, preferred_element_type=jnp.float32
            )
            inner = both[:, (1 - g) * wide : (2 - g) * wide]
            for y in range(half):
                label = labels_ref[1 - g, pl.ds(me * width + first + y, 1), :]
                density, shown = at_cells(label, density_ref, materials, members)
                near = slice((g * half + y) * depth, (g * half + y + 1) * depth)
                edge = slice((c * half + y) * depth, (c * half + y + 1) * depth)
                for m in range(groups):
                    start = pl.multiple_of((me ^ m) * members, members)
                    near_left[pl.ds(start, members), near] = sources[m][c, 1 - g, first + y + 1]
                    left_ref[g, pl.ds(start, members), edge] = sources[m][c, g, first + y + 1]
                    at = (m * half + y) * members
                    put_images(
                        inner[at : at + members], shown, density, near_right, start, near, count
                    )

        part = part + correlate(near_left[...], near_right[...])
    part_ref[...] = part


def vmem_spec():
    return pl.BlockSpec(memory_space=pltpu.VMEM)


def smem_spec():
    return pl.BlockSpec(memory_space=pltpu.SMEM)


def pack_kernel(pairs, me_ref, *refs):
    blocks = refs[:pairs]
    comps, planes, reach, members, depth = blocks[0].shape
    labelled = len(refs) > pairs + 2
    outs = refs[pairs + labelled : pairs + labelled + 2]
    half = (reach - 2) // 2
    for out, up in ((outs[0], 1 - me_ref[1]), (outs[1], me_ref[1])):
        first = (1 - up) * half
        for i, block in enumerate(blocks):
            for c in range(comps):
                out[i * comps + c] = block[c, up * (planes - 1), pl.ds(first, half + 2)]
        if labelled:
            labels_ref = refs[pairs]
            for y in range(half + 2):
                at = me_ref[0] * 2 * half + first + min(y, half - 1)
                row = labels_ref[up * (planes - 1), pl.ds(at, 1), :]
                out[pairs * comps, y] = jnp.broadcast_to(row, (members, depth)).astype(jnp.float32).astype(out.dtype)
    if labelled:
        put_stencil(refs[-1], planes)


def pack(pair, labels, me):
    comps, planes, reach, members, depth = pair[0].shape
    extra = [] if labels is None else [labels]
    out = jax.ShapeDtypeStruct(
        (len(pair) * comps + len(extra), (reach - 2) // 2 + 2, members, depth), pair[0].dtype
    )
    outs = [out, out]
    if extra:
        outs.append(jax.ShapeDtypeStruct((3 * planes * depth, 2 * planes * depth), pair[0].dtype))
    return pl.pallas_call(
        functools.partial(pack_kernel, len(pair)),
        out_shape=outs,
        in_specs=[smem_spec()] + [vmem_spec()] * (len(pair) + len(extra)),
        out_specs=[vmem_spec()] * len(outs),
        compiler_params=pltpu.CompilerParams(vmem_limit_bytes=16 * 2**20),
        cost_estimate=pl.CostEstimate(flops=0, bytes_accessed=2**20, transcendentals=0),
    )(me, *pair, *extra)


def local_tiles(blocks, labels, density, weights, me):
    groups = len(blocks)
    comps, planes, reach, members, depth = blocks[0].shape
    half = (reach - 2) // 2
    count = groups * members
    columns = (density.shape[0] + 1) * count
    image = jax.ShapeDtypeStruct((comps, 2, groups * half * members, 2 * depth), jnp.float32)
    return pl.pallas_call(
        functools.partial(local_kernel, groups, density.shape[0]),
        out_shape=[
            jax.ShapeDtypeStruct((count, columns), jnp.float32),
            image,
            image,
            jax.ShapeDtypeStruct((2, count, comps * half * depth), jnp.bfloat16),
        ],
        in_specs=[smem_spec(), smem_spec()] + [vmem_spec()] * (groups + 2),
        out_specs=[vmem_spec()] * 4,
        scratch_shapes=[
            pltpu.VMEM((count, 2 * half * depth), jnp.bfloat16),
            pltpu.VMEM((columns, 2 * half * depth), jnp.bfloat16),
        ]
        * comps,
        compiler_params=pltpu.CompilerParams(vmem_limit_bytes=40 * 2**20),
        cost_estimate=pl.CostEstimate(flops=5 * 10**9, bytes_accessed=12 * 2**20, transcendentals=0),
    )(me, density, *blocks, labels, weights)


def received_at(side, m, comps, c):
    part = 0
    while m >= side[part].shape[0] // comps:
        m -= side[part].shape[0] // comps
        part += 1
    return side[part].at[m * comps + c]


def returns_kernel(groups, materials, pairs, side, me_ref, density_ref, cross_ref, *refs):
    parts = refs[:pairs]
    back_ref, scratch = refs[pairs], refs[pairs + 1 :]
    me = me_ref[0]
    comps = cross_ref.shape[0]
    reach, members, depth = parts[0].shape[1:]
    half = reach - 2
    count = groups * members

    total = 0.0
    g = me_ref[1] if side else 1 - me_ref[1]
    for c in range(comps):
        left, right = scratch[2 * c : 2 * c + 2]
        cross = cross_ref[c, g]
        for y in range(half):
            label = parts[0][parts[0].shape[0] - 1, y].astype(jnp.float32)
            density, shown = at_cells(label, density_ref, materials, members)
            lanes = slice(y * depth, (y + 1) * depth)
            for m in range(groups):
                start = pl.multiple_of((me ^ m) * members, members)
                left[pl.ds(start, members), lanes] = received_at(parts, m, comps, c)[y + 1]
                at = (m * half + y) * members
                put_images(cross[at : at + members], shown, density, right, start, lanes, count)

        total = total + correlate(left[...], right[...])
    back_ref[...] = total


def return_tiles(cross, parts, side, density, me, groups):
    materials = density.shape[0]
    comps = cross.shape[0]
    reach, members, depth = parts[0].shape[1:]
    count = groups * members
    cells = comps * (reach - 2) * depth
    columns = (materials + 1) * count
    part = jax.ShapeDtypeStruct((count, columns), jnp.float32)
    return pl.pallas_call(
        functools.partial(returns_kernel, groups, materials, len(parts), side),
        out_shape=part,
        in_specs=[smem_spec(), smem_spec()] + [vmem_spec()] * (1 + len(parts)),
        out_specs=vmem_spec(),
        scratch_shapes=[
            pltpu.VMEM((count, cells // comps), jnp.bfloat16),
            pltpu.VMEM((columns, cells // comps), jnp.bfloat16),
        ]
        * comps,
        compiler_params=pltpu.CompilerParams(vmem_limit_bytes=40 * 2**20),
        cost_estimate=pl.CostEstimate(flops=3 * 10**9, bytes_accessed=6 * 2**20, transcendentals=0),
    )(me, density, cross, *parts)


def edge_kernel(groups, materials, pairs, me_ref, density_ref, near_ref, edge_ref, left_ref, *refs):
    sides = (refs[:pairs], refs[pairs : 2 * pairs])
    labels_ref, weights_ref, part_ref = refs[2 * pairs : 2 * pairs + 3]
    rights = refs[2 * pairs + 3 :]
    me = me_ref[0]
    comps = edge_ref.shape[0]
    reach, members, depth = sides[0][0].shape[1:]
    half = reach - 2
    width = 2 * half
    count = groups * members

    part = near_ref[...]
    for c in range(comps):
        for side in range(2):
            right = rights[2 * c + side]
            g = me_ref[1] if side else 1 - me_ref[1]
            lhs = jnp.concatenate(
                [
                    jnp.concatenate(three_rows(received_at(sides[side], m, comps, c), 0, half), axis=1)
                    for m in range(groups)
                ],
                axis=0,
            )
            image = edge_ref[c, g] + jnp.dot(lhs, weights_ref[3 * depth : 6 * depth, : 2 * depth], preferred_element_type=jnp.float32)
            for y in range(half):
                label = labels_ref[g, pl.ds(me * width + g * half + y, 1), :]
                density, shown = at_cells(label, density_ref, materials, members)
                lanes = slice(y * depth, (y + 1) * depth)
                for m in range(groups):
                    start = pl.multiple_of((me ^ m) * members, members)
                    at = (m * half + y) * members
                    put_images(image[at : at + members], shown, density, right, start, lanes, count)

            part = part + correlate(left_ref[g, :, c * half * depth : (c + 1) * half * depth], right[...])
    part_ref[...] = part


def combine_kernel(part_ref, below_ref, above_ref, from_below_ref, from_above_ref, slab_ref, wide_ref):
    count = part_ref.shape[0]
    copies = wide_ref.shape[0] // count
    part = part_ref[...]
    slab_ref[...] = part + (from_below_ref[...] + from_above_ref[...])
    total = part + (below_ref[...] + above_ref[...])
    depth = wide_ref.shape[2]
    for s in range(count):
        pieces = [total[s : s + 1, i * depth : (i + 1) * depth] for i in range(wide_ref.shape[1])]
        sent = jnp.concatenate(pieces, axis=0).astype(wide_ref.dtype)
        for r in range(copies):
            wide_ref[s * copies + r] = sent


def combine(part, returns, copies):
    count, columns = part.shape
    return pl.pallas_call(
        combine_kernel,
        out_shape=[
            jax.ShapeDtypeStruct((count, columns), jnp.float32),
            jax.ShapeDtypeStruct((count * copies, columns // 128, 128), jnp.bfloat16),
        ],
        in_specs=[vmem_spec()] * (1 + len(returns)),
        out_specs=[vmem_spec()] * 2,
        compiler_params=pltpu.CompilerParams(vmem_limit_bytes=16 * 2**20),
        cost_estimate=pl.CostEstimate(flops=0, bytes_accessed=2**19, transcendentals=0),
    )(part, *returns)


def edge_tiles(near, edge, left, lows, highs, labels, density, weights, me, groups):
    count, columns = near.shape
    materials = density.shape[0]
    part = jax.ShapeDtypeStruct((count, columns), jnp.float32)
    halos = [*lows, *highs]
    return pl.pallas_call(
        functools.partial(edge_kernel, groups, materials, len(lows)),
        out_shape=part,
        in_specs=[smem_spec(), smem_spec()] + [vmem_spec()] * (5 + len(halos)),
        out_specs=vmem_spec(),
        scratch_shapes=[pltpu.VMEM((columns, left.shape[2] // edge.shape[0]), jnp.bfloat16)] * (2 * edge.shape[0]),
        compiler_params=pltpu.CompilerParams(vmem_limit_bytes=40 * 2**20),
        cost_estimate=pl.CostEstimate(flops=5 * 10**9, bytes_accessed=20 * 2**20, transcendentals=0),
    )(me, density, near, edge, left, *halos, labels, weights)


def finish_kernel(count, slab_scale, gram_scale, *refs):
    parts, rows_ref, slab_ref, gram_ref = refs[:-3], refs[-3], refs[-2], refs[-1]
    terms = [p[...] for p in parts]
    while len(terms) > 1:
        terms = [terms[i] + terms[i + 1] for i in range(0, len(terms), 2)]
    slab = terms[0] * slab_scale
    gram = jnp.sum(rows_ref[...].astype(jnp.float32), axis=0) * gram_scale
    across = gram.shape[1] // count
    for j in range(slab.shape[1] // count):
        slab_ref[0, j] = slab[:, j * count : (j + 1) * count]
        gram_ref[j] = gram[j // across : j // across + 1, j % across * count : (j % across + 1) * count]


def finish(parts, rows, slab_scale, gram_scale):
    count, columns = parts[0].shape
    blocks = columns // count
    return pl.pallas_call(
        functools.partial(finish_kernel, count, slab_scale, gram_scale),
        out_shape=[
            jax.ShapeDtypeStruct((1, blocks, count, count), jnp.float32),
            jax.ShapeDtypeStruct((blocks, 1, count), jnp.float32),
        ],
        in_specs=[vmem_spec()] * (1 + len(parts)),
        out_specs=[vmem_spec()] * 2,
        compiler_params=pltpu.CompilerParams(vmem_limit_bytes=16 * 2**20),
    )(*parts, rows)


def body(snapshots, labels, free_mask, density):
    groups, slabs = lax.axis_size("snap"), lax.axis_size("space")
    planes, rows, depth = labels.shape
    me = jnp.stack([lax.axis_index("snap"), lax.axis_index("space") % 2]).astype(jnp.int32)
    with jax.named_scope("spread"):
        mine = spread(snapshots, free_mask, lax.axis_index("snap").astype(jnp.int32).reshape(1), groups)
    with jax.named_scope("regroup"):
        blocks = [mine[0]] + [
            lax.ppermute(mine[m], "snap", [(i, i ^ m) for i in range(groups)]) for m in range(1, groups)
        ]
    with jax.named_scope("halo"):
        even = [(i, i ^ 1) for i in range(slabs)]
        odd = [(i, ((i + 1) ^ 1) - 1) for i in range(1, slabs - 1)]
        firsts, seconds = [], []
        for start in range(0, groups, 2):
            some = blocks[start : start + 2]
            if firsts:
                some, *_ = lax.optimization_barrier((some, to_even, to_odd))
            to_even, to_odd, *stencil = pack(some, None if firsts else labels, me)
            if firsts:
                some, to_odd = lax.optimization_barrier((some, to_odd))
                to_even, _ = pack(some, None, me)
            if not firsts:
                weights = stencil[0]
                some, to_even, to_odd = lax.optimization_barrier((some, to_even, to_odd))
            seconds.append(lax.ppermute(to_odd, "space", odd))
            firsts.append(lax.ppermute(to_even, "space", even))
    with jax.named_scope("local_tiles"):
        near, edge, cross, left = local_tiles(blocks, labels, density, weights, me)
    with jax.named_scope("return_tiles"):
        above = return_tiles(cross, seconds, 1, density, me, groups)
        from_above = lax.ppermute(above, "space", odd)
        firsts, above = lax.optimization_barrier((firsts, above))
        below = return_tiles(cross, firsts, 0, density, me, groups)
        from_below = lax.ppermute(below, "space", even)
    with jax.named_scope("edge_tiles"):
        part = edge_tiles(near, edge, left, firsts, seconds, labels, density, weights, me, groups)
    with jax.named_scope("sums"):
        part, wide = combine(part, (below, above, from_below, from_above), groups)
        sent = lax.all_to_all(wide, ("space", "snap"), 0, 0, tiled=True)
        parts = [part] + [
            lax.ppermute(part, "snap", [(i, i ^ m) for i in range(groups)]) for m in range(1, groups)
        ]
        slab_scale = 1.0 / (3.0 * planes * rows * depth)
        slab, gram = finish(parts, sent, slab_scale, slab_scale / slabs)
    return gram, slab


def solution(mesh):
    in_specs = (
        P("snap", None, "space", None, None),
        P("space", None, None),
        P("space", None, None),
        P(),
    )
    out_specs = (P(None, "space", None), P("space", None, None, None))
    return jax.shard_map(body, mesh=mesh, in_specs=in_specs, out_specs=out_specs, check_vma=False)
```
